512 devices in a mesh: row: 16 (over y_hi, x, core), col: 32 (over y_lo, z).
Axes of the slice: x: 4, y: 8 (y_hi: 2, y_lo: 4; y = y_hi * 4 + y_lo), z: 8, core: 2. Of those that a mesh axis runs over, the one named last changes fastest.
Arguments:
- samples: bfloat16 [256, 16384], P('row', 'col'), may hold values from -40 to 40
- counts: int32 [256], replicated, may hold values from 1 to 64
- shrink_num: int32 [1], replicated, may hold values from 20 to 60
- shrink_den: int32 [1], replicated, may hold values from 100 to 128
Outputs:
- factored: float32 [2, 8192, 16384], P(None, 'row', 'col')
The draws below stay inside these ranges and needn't reach their ends.
All inputs are finite; a program needn't handle non-finite values.
Results may differ from the reference program's by a relative error of at most 0.0048.
Values may be sent and summed in bfloat16 or wider, within the bound.
No kernel may reach another device: no remote copies, remote signals or barrier semaphores. Data moves between devices by JAX's collectives and lax.ppermute only.
A program may use at most 64 MiB of HBM per device.

```python
import math
import jax
import jax.numpy as jnp
from jax import lax

TILE_WIDTH = 512
SAMPLES = 256
FEATURES = 16384
N_ROW = 16
N_COL = 32


def draw_samples(key, part):
    key = jax.random.fold_in(key, 7)
    first, second = jax.random.split(key, 2)
    position = jnp.arange(FEATURES, dtype=jnp.float32) / FEATURES
    rough = jnp.exp(jax.random.uniform(second, (FEATURES,), minval=0.0, maxval=math.log(3.2)))
    spread = 0.45 * jnp.exp(0.5 * math.log(3.0) * position) * rough
    values = jnp.clip(jax.random.normal(first, (SAMPLES, FEATURES)), -6.0, 6.0) * spread
    return values.astype(jnp.float32).astype(jnp.bfloat16)


def touch_ends(array, key, low, top_value):
    extent = array.shape
    index_at = [jax.random.randint(jax.random.fold_in(key, axis), (), 0, extent[axis]) for axis in range(len(extent))]
    array = array.at[tuple(index_at)].set(low)
    longest = extent.index(max(extent))
    index_at[longest] = (index_at[longest] + 1) % extent[longest]
    return array.at[tuple(index_at)].set(top_value)


def setup_inputs(seed: int = 0) -> dict:
    key_list = jax.random.split(jax.random.key(seed), 5)
    samples = draw_samples(jax.random.fold_in(key_list[4], 71), 0)
    counts = touch_ends(jax.random.randint(key_list[1], (SAMPLES,), 1, 65), jax.random.fold_in(key_list[1], 1), 1, 64).astype(jnp.int32)
    shrink_num = jax.random.randint(key_list[2], (1,), 20, 61).astype(jnp.int32)
    shrink_den = jax.random.randint(key_list[3], (1,), 100, 129).astype(jnp.int32)
    return {"samples": samples, "counts": counts, "shrink_num": shrink_num, "shrink_den": shrink_den}


def reference(samples, counts, shrink_num, shrink_den):
    weights = counts.astype(jnp.float32) / jnp.sum(counts.astype(jnp.float32))
    shrinkage = shrink_num[0].astype(jnp.float32) / shrink_den[0].astype(jnp.float32)
    values = samples.astype(jnp.float32)
    mean = lax.optimization_barrier(jnp.sum(weights[:, None] * values, axis=0))
    scaled = (jnp.sqrt(weights)[:, None] * (values - mean)).astype(jnp.bfloat16)
    level = shrinkage * jnp.sum(jnp.square(scaled.astype(jnp.float32))) / FEATURES
    width = TILE_WIDTH
    panel = (1.0 - shrinkage) * jnp.dot(scaled.T.astype(jnp.float32), scaled[:, :width].astype(jnp.float32), preferred_element_type=jnp.float32)
    panel = panel + level * jnp.eye(FEATURES, width, dtype=jnp.float32)
    diag_factor = jnp.linalg.cholesky(panel[:width, :width])
    below = lax.linalg.triangular_solve(diag_factor, panel[width:, :width], left_side=False, lower=True, transpose_a=True)
    panel = jnp.concatenate([diag_factor, below], axis=0)

    def one_row(tile_row):
        first = tile_row * TILE_WIDTH
        row_scaled = lax.dynamic_slice_in_dim(scaled, first, TILE_WIDTH, 1)
        positions = jnp.arange(FEATURES, dtype=jnp.int32)[None, :]
        targets = first + jnp.arange(TILE_WIDTH, dtype=jnp.int32)[:, None]
        block = (1.0 - shrinkage) * jnp.dot(row_scaled.T.astype(jnp.float32), scaled.astype(jnp.float32), preferred_element_type=jnp.float32)
        block = block + jnp.where(positions == targets, level, 0.0)
        left_rows = lax.dynamic_slice_in_dim(panel, first, TILE_WIDTH, 0)
        rest = block - jnp.dot(left_rows, panel.T, precision=lax.Precision.HIGHEST)
        rest = jnp.where(tile_row < 1, 0.0, rest)
        return jnp.concatenate([left_rows, rest[:, width:]], axis=1)
    rows = lax.map(one_row, jnp.arange(FEATURES // TILE_WIDTH, dtype=jnp.int32))
    return rows.reshape(N_COL // N_ROW, N_ROW * TILE_WIDTH, FEATURES)
```

```python
import functools

import jax
import jax.numpy as jnp
from jax import lax
from jax.experimental import pallas as pl
from jax.experimental.pallas import tpu as pltpu
from jax.sharding import PartitionSpec as P

BLOCK = 128
MICRO = 32
F32 = jnp.float32
BF16 = jnp.bfloat16
VMEM = pl.BlockSpec(memory_space=pltpu.VMEM)
SMEM = pl.BlockSpec(memory_space=pltpu.SMEM)


def dot(left, right, dims, precision=None):
    return lax.dot_general(
        left, right, ((dims[0], dims[1]), ((), ())),
        precision=precision, preferred_element_type=F32,
    )


def exact_dot(left, right, dims):
    return dot(left, right, dims, lax.Precision.HIGHEST)


def split(value):
    high = value.astype(BF16)
    return high, (value - high.astype(F32)).astype(BF16)


def scale_kernel(place_ref, counts_ref, samples_ref, scaled_ref, pieces_ref):
    count, rows, width = samples_ref.shape
    number = count * rows
    counts = counts_ref[...].astype(F32)
    weights = jnp.broadcast_to(counts / jnp.sum(counts), (8, number))
    column = jnp.transpose(weights)[:, 0:1]
    values = samples_ref[...].reshape(number, width).astype(F32)
    mean = jnp.sum(column * values, axis=0, keepdims=True)
    scaled = (jnp.sqrt(column) * (values - mean)).astype(BF16)
    scaled_ref[...] = scaled
    share = jnp.sum(jnp.square(scaled.astype(F32)), axis=0, keepdims=True)
    share = jnp.broadcast_to(jnp.sum(share, axis=1, keepdims=True), (rows, 128))
    high, rest = split(share)
    middle = rest
    low = (share - high.astype(F32) - middle.astype(F32)).astype(BF16)
    line = lax.broadcasted_iota(jnp.int32, (rows, 128), 0)
    tail = jnp.where(line == 0, high.astype(F32), 0.0)
    tail = jnp.where(line == 1, middle.astype(F32), tail)
    tail = jnp.where(line == 2, low.astype(F32), tail).astype(BF16)
    first = pl.multiple_of(place_ref[0] * rows, rows)
    own = scaled_ref[pl.ds(first, rows), :]
    for target in range(pieces_ref.shape[0]):
        pieces_ref[target, :, 0:width] = own
        pieces_ref[target, :, width:] = tail


def deal_kernel(pieces_ref, dealt_ref, trace_ref):
    columns, rows, _ = pieces_ref.shape
    targets, _, width = dealt_ref.shape
    for target in range(targets):
        dealt_ref[target, 0:rows, :] = pieces_ref[0, :, 0:width]
        for position in range(columns // targets):
            tile = position * targets + target
            dealt_ref[target, (position + 1) * rows:(position + 2) * rows, :] = pieces_ref[tile, :, 0:width]
    tails = pieces_ref[:, :, width:].reshape(columns * rows, 128).astype(F32)
    total = jnp.sum(tails, axis=0, keepdims=True)
    trace_ref[...] = jnp.broadcast_to(total, (8, 128))


def eliminate(work_ref, first, micro):
    lanes = work_ref.shape[1]
    groups = micro // 8
    rows = [[work_ref[first + 8 * g:first + 8 * g + 8, 128 * w:128 * w + 128] for w in range(lanes // 128)] for g in range(groups)]
    part, lane = first // 128, first % 128
    columns = [
        [jnp.broadcast_to(rows[g][part][:, lane + k:lane + k + 1], (8, 128)) for g in range(groups)] for k in range(micro)
    ]
    for j in range(micro):
        group, line = j // 8, j % 8

        def spread(value):
            return jnp.broadcast_to(value[line:line + 1, :], (8, 128))

        scale = lax.rsqrt(spread(columns[j][group]))
        multiplier = [columns[j][g] * scale for g in range(groups)]
        for k in range(j + 1, micro):
            pivot = spread(columns[k][group]) * scale
            for g in range((j + 1) // 8, groups):
                columns[k][g] = columns[k][g] - multiplier[g] * pivot
        for w in range(lanes // 128):
            pivot = spread(rows[group][w]) * scale
            work_ref[first + j:first + j + 1, 128 * w:128 * w + 128] = pivot[0:1, :]
            for g in range((j + 1) // 8, groups):
                rows[g][w] = rows[g][w] - multiplier[g] * pivot


def factor_block(work_ref, block, micro):
    for first in range(0, block, micro):
        eliminate(work_ref, first, micro)
        after = first + micro
        if after < block:
            panel = work_ref[first:after, :]
            work_ref[after:, :] = work_ref[after:, :] - exact_dot(panel[:, after:block], panel, ((0,), (0,)))


def identity(size):
    return jnp.where(
        lax.broadcasted_iota(jnp.int32, (size, size), 0) == lax.broadcasted_iota(jnp.int32, (size, size), 1), 1.0, 0.0
    ).astype(F32)


def factor_kernel(place_ref, shrink_ref, trace_ref, scaled_ref, dealt_ref, out_ref, panel_ref, work_ref):
    sources, dealt_rows, width = dealt_ref.shape
    samples = scaled_ref.shape[0]
    rows = samples // sources
    positions = out_ref.shape[0]
    row_index, col_index, taps = place_ref[0], place_ref[1], place_ref[2]
    shrinkage = shrink_ref[0].astype(F32) / shrink_ref[1].astype(F32)
    keep = 1.0 - shrinkage
    level = shrinkage * trace_ref[0:1, 0:1] / taps.astype(F32)
    first_tile = dealt_ref[:, 0:rows, :].reshape(samples, width)
    panel_ref[:, 0:width] = keep * dot(first_tile, first_tile, ((0,), (0,))) + level * identity(width)
    panel_ref[:, width:] = jnp.transpose(first_tile.astype(F32))
    for start in range(0, width, BLOCK):
        stop = start + BLOCK
        work_ref[:, 0:BLOCK] = panel_ref[start:stop, start:stop]
        work_ref[:, BLOCK:] = identity(BLOCK)
        factor_block(work_ref, BLOCK, MICRO)
        panel_ref[start:stop, start:stop] = work_ref[:, 0:BLOCK]
        done = exact_dot(work_ref[:, BLOCK:], panel_ref[start:stop, stop:], ((1,), (0,)))
        panel_ref[start:stop, stop:] = done
        if stop < width:
            panel_ref[stop:width, stop:] = panel_ref[stop:width, stop:] - exact_dot(done[:, 0:width - stop], done, ((0,), (0,)))
    reduced = panel_ref[:, width:]

    def finish(right):
        right_high, right_low = split(right)
        for position in range(positions):
            tile = dealt_ref[:, (position + 1) * rows:(position + 2) * rows, :].reshape(samples, width)
            product = dot(tile, right_high, ((0,), (0,))) + dot(tile, right_low, ((0,), (0,)))
            out_ref[position] = keep * product

    @pl.when(col_index == 0)
    def _():
        finish(jnp.transpose(reduced))

    @pl.when(col_index > 0)
    def _():
        high, low = split(reduced)
        inner = dot(high, high, ((0,), (0,))) + dot(high, low, ((0,), (0,))) + dot(low, high, ((0,), (0,)))
        inner_high, inner_low = split(inner)
        own = scaled_ref[...]
        removed = dot(inner_high, own, ((1,), (0,))) + dot(inner_low, own, ((1,), (0,)))
        finish(own.astype(F32) - keep * removed)
        for position in range(positions):
            @pl.when(position * sources + row_index == col_index)
            def _():
                out_ref[position] = out_ref[position] + level * identity(width)

    @pl.when((row_index == 0) & (col_index > 0))
    def _():
        out_ref[0] = jnp.zeros((width, width), F32)

    @pl.when((row_index == 0) & (col_index == 0))
    def _():
        upper = panel_ref[:, 0:width]
        line = lax.broadcasted_iota(jnp.int32, (width, width), 0)
        lane = lax.broadcasted_iota(jnp.int32, (width, width), 1)
        out_ref[0] = jnp.transpose(jnp.where(line <= lane, upper, 0.0))


def scale(place, counts, gathered, columns):
    count, rows, width = gathered.shape
    return pl.pallas_call(
        scale_kernel,
        out_shape=(
            jax.ShapeDtypeStruct((count * rows, width), BF16),
            jax.ShapeDtypeStruct((columns, rows, width + 128), BF16),
        ),
        in_specs=[SMEM, VMEM, VMEM],
        out_specs=(VMEM, VMEM),
        compiler_params=pltpu.CompilerParams(vmem_limit_bytes=32 * 2**20),
    )(place, counts[None, :], gathered)


def deal(pieces, targets):
    columns, rows, wide = pieces.shape
    return pl.pallas_call(
        deal_kernel,
        out_shape=(
            jax.ShapeDtypeStruct((targets, (1 + columns // targets) * rows, wide - 128), BF16),
            jax.ShapeDtypeStruct((8, 128), F32),
        ),
        in_specs=[VMEM],
        out_specs=(VMEM, VMEM),
        compiler_params=pltpu.CompilerParams(vmem_limit_bytes=32 * 2**20),
    )(pieces)


def factor(place, shrink, trace, scaled, dealt):
    samples, width = scaled.shape
    positions = dealt.shape[1] * dealt.shape[0] // samples - 1
    return pl.pallas_call(
        factor_kernel,
        out_shape=jax.ShapeDtypeStruct((positions, width, width), F32),
        in_specs=[SMEM, SMEM, VMEM, VMEM, VMEM],
        out_specs=VMEM,
        scratch_shapes=[
            pltpu.VMEM((width, width + samples), F32),
            pltpu.VMEM((BLOCK, 2 * BLOCK), F32),
        ],
        compiler_params=pltpu.CompilerParams(vmem_limit_bytes=48 * 2**20),
    )(place, shrink, trace, scaled, dealt)


def per_device(samples, counts, shrink_num, shrink_den):
    rows_count = lax.axis_size("row")
    cols_count = lax.axis_size("col")
    rows, width = samples.shape
    place = jnp.stack(
        [lax.axis_index("row"), lax.axis_index("col"), jnp.int32(width * cols_count)]
    ).astype(jnp.int32)
    shrink = jnp.concatenate([shrink_num, shrink_den])
    copies = jnp.broadcast_to(samples[None], (rows_count, rows, width))
    gathered = lax.all_to_all(copies, "row", 0, 0)
    scaled, pieces = scale(place, counts, gathered, cols_count)
    exchanged = lax.all_to_all(pieces, "col", 0, 0)
    dealt, trace = deal(exchanged, rows_count)
    dealt = lax.all_to_all(dealt, "row", 0, 0)
    return factor(place, shrink, trace, scaled, dealt)


def solution(mesh):
    in_specs = (P("row", "col"), P(), P(), P())
    out_specs = P(None, "row", "col")
    return jax.shard_map(
        per_device, mesh=mesh, in_specs=in_specs, out_specs=out_specs, check_vma=False
    )
```

```python
import jax
import jax.numpy as jnp
from jax import lax
from jax.experimental import pallas as pl
from jax.experimental.pallas import tpu as pltpu
from jax.sharding import PartitionSpec as P

BLOCK = 128
MICRO = 32
F32 = jnp.float32
BF16 = jnp.bfloat16
VMEM = pl.BlockSpec(memory_space=pltpu.VMEM)
SMEM = pl.BlockSpec(memory_space=pltpu.SMEM)


def dot(left, right, dims, precision=None):
    return lax.dot_general(
        left, right, ((dims[0], dims[1]), ((), ())),
        precision=precision, preferred_element_type=F32,
    )


def exact_dot(left, right, dims):
    return dot(left, right, dims, lax.Precision.HIGHEST)


def split(value):
    high = value.astype(BF16)
    return high, (value - high.astype(F32)).astype(BF16)


def scale_kernel(place_ref, counts_ref, samples_ref, scaled_ref, pieces_ref):
    count, rows, width = samples_ref.shape
    number = count * rows
    counts = counts_ref[...].astype(F32)
    weights = jnp.broadcast_to(counts / jnp.sum(counts), (8, number))
    column = jnp.transpose(weights)[:, 0:1]
    values = samples_ref[...].reshape(number, width).astype(F32)
    mean = jnp.sum(column * values, axis=0, keepdims=True)
    scaled = (jnp.sqrt(column) * (values - mean)).astype(BF16)
    scaled_ref[...] = scaled
    share = jnp.sum(jnp.square(scaled.astype(F32)), axis=0, keepdims=True)
    share = jnp.broadcast_to(jnp.sum(share, axis=1, keepdims=True), (rows, 128))
    high, rest = split(share)
    middle = rest
    low = (share - high.astype(F32) - middle.astype(F32)).astype(BF16)
    line = lax.broadcasted_iota(jnp.int32, (rows, 128), 0)
    tail = jnp.where(line == 0, high.astype(F32), 0.0)
    tail = jnp.where(line == 1, middle.astype(F32), tail)
    tail = jnp.where(line == 2, low.astype(F32), tail).astype(BF16)
    first = pl.multiple_of(place_ref[0] * rows, rows)
    own = scaled_ref[pl.ds(first, rows), :]
    for target in range(pieces_ref.shape[0]):
        pieces_ref[target, :, 0:width] = own
        pieces_ref[target, :, width:] = tail


def deal_kernel(pieces_ref, dealt_ref, trace_ref):
    columns, rows, _ = pieces_ref.shape
    targets, _, width = dealt_ref.shape
    for target in range(targets):
        dealt_ref[target, 0:rows, :] = pieces_ref[0, :, 0:width]
        for position in range(columns // targets):
            tile = position * targets + target
            dealt_ref[target, (position + 1) * rows:(position + 2) * rows, :] = pieces_ref[tile, :, 0:width]
    tails = pieces_ref[:, :, width:].reshape(columns * rows, 128).astype(F32)
    total = jnp.sum(tails, axis=0, keepdims=True)
    trace_ref[...] = jnp.broadcast_to(total, (8, 128))


def eliminate(work_ref, first, micro):
    lanes = work_ref.shape[1]
    groups = micro // 8
    rows = [[work_ref[first + 8 * g:first + 8 * g + 8, 128 * w:128 * w + 128] for w in range(lanes // 128)] for g in range(groups)]
    part, lane = first // 128, first % 128
    columns = [
        [jnp.broadcast_to(rows[g][part][:, lane + k:lane + k + 1], (8, 128)) for g in range(groups)] for k in range(micro)
    ]
    for j in range(micro):
        group, line = j // 8, j % 8

        def spread(value):
            return jnp.broadcast_to(value[line:line + 1, :], (8, 128))

        scale = lax.rsqrt(spread(columns[j][group]))
        multiplier = [columns[j][g] * scale for g in range(groups)]
        for k in range(j + 1, micro):
            pivot = spread(columns[k][group]) * scale
            for g in range((j + 1) // 8, groups):
                columns[k][g] = columns[k][g] - multiplier[g] * pivot
        for w in range(lanes // 128):
            pivot = spread(rows[group][w]) * scale
            work_ref[first + j:first + j + 1, 128 * w:128 * w + 128] = pivot[0:1, :]
            for g in range((j + 1) // 8, groups):
                rows[g][w] = rows[g][w] - multiplier[g] * pivot


def factor_block(work_ref, block, micro):
    for first in range(0, block, micro):
        eliminate(work_ref, first, micro)
        after = first + micro
        if after < block:
            panel = work_ref[first:after, :]
            work_ref[after:, :] = work_ref[after:, :] - exact_dot(panel[:, after:block], panel, ((0,), (0,)))


def identity(size):
    return jnp.where(
        lax.broadcasted_iota(jnp.int32, (size, size), 0) == lax.broadcasted_iota(jnp.int32, (size, size), 1), 1.0, 0.0
    ).astype(F32)


def factor_panel(panel_ref, work_ref, order):
    for start in range(0, order, BLOCK):
        stop = start + BLOCK
        work_ref[:, 0:BLOCK] = panel_ref[start:stop, start:stop]
        work_ref[:, BLOCK:] = identity(BLOCK)
        factor_block(work_ref, BLOCK, MICRO)
        panel_ref[start:stop, start:stop] = work_ref[:, 0:BLOCK]
        done = exact_dot(work_ref[:, BLOCK:], panel_ref[start:stop, stop:], ((1,), (0,)))
        panel_ref[start:stop, stop:] = done
        if stop < order:
            panel_ref[stop:order, stop:] = panel_ref[stop:order, stop:] - exact_dot(done[:, 0:order - stop], done, ((0,), (0,)))


def coefficients(place_ref, shrink_ref, trace_ref):
    shrinkage = shrink_ref[0].astype(F32) / shrink_ref[1].astype(F32)
    return 1.0 - shrinkage, shrinkage * trace_ref[0:1, 0:1] / place_ref[2].astype(F32)


def panel_kernel(place_ref, shrink_ref, trace_ref, scaled_ref, below_ref, diagonal_ref, panel_ref, work_ref):
    width = scaled_ref.shape[1]

    @pl.when(place_ref[1] == 0)
    def _():
        keep, level = coefficients(place_ref, shrink_ref, trace_ref)
        own = scaled_ref[...]
        panel_ref[:, 0:width] = (keep / level) * dot(own, own, ((0,), (0,))) + identity(width)
        panel_ref[:, width:] = jnp.transpose(own.astype(F32))
        factor_panel(panel_ref, work_ref, width)
        root = jnp.sqrt(level)
        below_ref[...] = jnp.transpose(panel_ref[:, width:]) * (keep / root)
        line = lax.broadcasted_iota(jnp.int32, (width, width), 0)
        lane = lax.broadcasted_iota(jnp.int32, (width, width), 1)
        diagonal_ref[...] = jnp.transpose(jnp.where(line <= lane, panel_ref[:, 0:width], 0.0)) * root


def tiles_kernel(place_ref, shrink_ref, trace_ref, scaled_ref, below_ref, diagonal_ref, dealt_ref, out_ref, panel_ref, work_ref):
    sources, _, width = dealt_ref.shape
    samples = scaled_ref.shape[0]
    rows = samples // sources
    positions = out_ref.shape[0]
    row_index, col_index = place_ref[0], place_ref[1]
    keep, level = coefficients(place_ref, shrink_ref, trace_ref)

    def finish(right):
        right_high, right_low = split(right)
        for position in range(positions):
            tile = dealt_ref[:, (position + 1) * rows:(position + 2) * rows, :].reshape(samples, width)
            out_ref[position] = dot(tile, right_high, ((0,), (0,))) + dot(tile, right_low, ((0,), (0,)))

    @pl.when(col_index == 0)
    def _():
        finish(below_ref[...])

    @pl.when(col_index > 0)
    def _():
        first_tile = dealt_ref[:, 0:rows, :].reshape(samples, width)
        panel_ref[:, 0:samples] = (keep / level) * dot(first_tile, first_tile, ((1,), (1,))) + identity(samples)
        panel_ref[:, samples:] = identity(samples)
        factor_panel(panel_ref, work_ref, samples)
        inverse_factor = panel_ref[:, samples:]
        high, low = split(keep * exact_dot(inverse_factor, inverse_factor, ((0,), (0,))))
        own = scaled_ref[...]
        finish(dot(high, own, ((1,), (0,))) + dot(low, own, ((1,), (0,))))
        for position in range(positions):
            @pl.when(position * sources + row_index == col_index)
            def _():
                out_ref[position] = out_ref[position] + level * identity(width)

    @pl.when((row_index == 0) & (col_index > 0))
    def _():
        out_ref[0] = jnp.zeros((width, width), F32)

    @pl.when((row_index == 0) & (col_index == 0))
    def _():
        out_ref[0] = diagonal_ref[...]


def scale(place, counts, gathered, columns):
    count, rows, width = gathered.shape
    return pl.pallas_call(
        scale_kernel,
        out_shape=(
            jax.ShapeDtypeStruct((count * rows, width), BF16),
            jax.ShapeDtypeStruct((columns, rows, width + 128), BF16),
        ),
        in_specs=[SMEM, VMEM, VMEM],
        out_specs=(VMEM, VMEM),
        compiler_params=pltpu.CompilerParams(vmem_limit_bytes=32 * 2**20),
    )(place, counts[None, :], gathered)


def deal(pieces, targets):
    columns, rows, wide = pieces.shape
    return pl.pallas_call(
        deal_kernel,
        out_shape=(
            jax.ShapeDtypeStruct((targets, (1 + columns // targets) * rows, wide - 128), BF16),
            jax.ShapeDtypeStruct((8, 128), F32),
        ),
        in_specs=[VMEM],
        out_specs=(VMEM, VMEM),
        compiler_params=pltpu.CompilerParams(vmem_limit_bytes=32 * 2**20),
    )(pieces)


def panel(place, shrink, trace, scaled):
    samples, width = scaled.shape
    return pl.pallas_call(
        panel_kernel,
        out_shape=(
            jax.ShapeDtypeStruct((samples, width), F32),
            jax.ShapeDtypeStruct((width, width), F32),
        ),
        in_specs=[SMEM, SMEM, VMEM, VMEM],
        out_specs=(VMEM, VMEM),
        scratch_shapes=[
            pltpu.VMEM((width, width + samples), F32),
            pltpu.VMEM((BLOCK, 2 * BLOCK), F32),
        ],
        compiler_params=pltpu.CompilerParams(vmem_limit_bytes=32 * 2**20),
        cost_estimate=pl.CostEstimate(flops=20 * 10**9, bytes_accessed=2 * 2**20, transcendentals=0),
    )(place, shrink, trace, scaled)


def tiles(place, shrink, trace, scaled, below, diagonal, dealt):
    samples, width = scaled.shape
    positions = dealt.shape[1] * dealt.shape[0] // samples - 1
    return pl.pallas_call(
        tiles_kernel,
        out_shape=jax.ShapeDtypeStruct((positions, width, width), F32),
        in_specs=[SMEM, SMEM] + [VMEM] * 5,
        out_specs=VMEM,
        scratch_shapes=[
            pltpu.VMEM((samples, 2 * samples), F32),
            pltpu.VMEM((BLOCK, 2 * BLOCK), F32),
        ],
        compiler_params=pltpu.CompilerParams(vmem_limit_bytes=32 * 2**20),
    )(place, shrink, trace, scaled, below, diagonal, dealt)


def per_device(samples, counts, shrink_num, shrink_den):
    rows_count = lax.axis_size("row")
    cols_count = lax.axis_size("col")
    rows, width = samples.shape
    place = jnp.stack(
        [lax.axis_index("row"), lax.axis_index("col"), jnp.int32(width * cols_count)]
    ).astype(jnp.int32)
    shrink = jnp.concatenate([shrink_num, shrink_den])
    copies = jnp.broadcast_to(samples[None], (rows_count, rows, width))
    gathered = lax.all_to_all(copies, "row", 0, 0)
    scaled, pieces = scale(place, counts, gathered, cols_count)
    exchanged = lax.all_to_all(pieces, "col", 0, 0)
    dealt, trace = deal(exchanged, rows_count)
    dealt = lax.all_to_all(dealt, "row", 0, 0)
    below, diagonal = panel(place, shrink, trace, scaled)
    return tiles(place, shrink, trace, scaled, below, diagonal, dealt)


def solution(mesh):
    in_specs = (P("row", "col"), P(), P(), P())
    out_specs = P(None, "row", "col")
    return jax.shard_map(
        per_device, mesh=mesh, in_specs=in_specs, out_specs=out_specs, check_vma=False
    )
```

```python
import functools

import jax
import jax.numpy as jnp
from jax import lax
from jax.experimental import pallas as pl
from jax.experimental.pallas import tpu as pltpu
from jax.sharding import PartitionSpec as P

BLOCK = 128
MICRO = 32
STRIP = 16
TAIL = 8
F32 = jnp.float32
BF16 = jnp.bfloat16
VMEM = pl.BlockSpec(memory_space=pltpu.VMEM)
SMEM = pl.BlockSpec(memory_space=pltpu.SMEM)


def dot(left, right, dims, precision=None):
    return lax.dot_general(
        left, right, ((dims[0], dims[1]), ((), ())),
        precision=precision, preferred_element_type=F32,
    )


def exact_dot(left, right, dims):
    return dot(left, right, dims, lax.Precision.HIGHEST)


def split(value):
    high = value.astype(BF16)
    return high, (value - high.astype(F32)).astype(BF16)


def copies_kernel(samples_ref, copies_ref):
    for target in range(copies_ref.shape[0]):
        copies_ref[target] = samples_ref[...]


def scale_kernel(counts_ref, samples_ref, scaled_ref, pieces_ref):
    count, rows, width = samples_ref.shape
    number = count * rows
    counts = counts_ref[...].astype(F32)
    weights = jnp.broadcast_to(counts / jnp.sum(counts), (8, number))
    column = jnp.transpose(weights)[:, 0:1]
    values = samples_ref[...].reshape(number, width).astype(F32)
    mean = jnp.sum(column * values, axis=0, keepdims=True)
    scaled = (jnp.sqrt(column) * (values - mean)).astype(BF16)
    scaled_ref[...] = scaled
    share = jnp.sum(jnp.square(scaled.astype(F32)), axis=0, keepdims=True)
    share = jnp.broadcast_to(jnp.sum(share, axis=1, keepdims=True), (TAIL, 128))
    high, middle = split(share)
    low = (share - high.astype(F32) - middle.astype(F32)).astype(BF16)
    line = lax.broadcasted_iota(jnp.int32, (TAIL, 128), 0)
    tail = jnp.where(line == 0, high.astype(F32), 0.0)
    tail = jnp.where(line == 1, middle.astype(F32), tail)
    tail = jnp.where(line == 2, low.astype(F32), tail).astype(BF16)
    first = pl.multiple_of(lax.axis_index("row") * rows, rows)
    own = scaled_ref[pl.ds(first, rows), :]
    body = pieces_ref.shape[1] - TAIL
    for target in range(pieces_ref.shape[0]):
        for part in range(width // 128):
            pieces_ref[target, part * rows:(part + 1) * rows, :] = own[:, part * 128:(part + 1) * 128]
        pieces_ref[target, body:, :] = tail


def deal_kernel(pieces_ref, dealt_ref, trace_ref):
    columns, high, _ = pieces_ref.shape
    targets, dealt_rows, width = dealt_ref.shape
    positions = columns // targets
    rows = dealt_rows // (1 + positions)
    for target in range(targets):
        tiles_of_target = [0] + [position * targets + target for position in range(positions)]
        for place, tile in enumerate(tiles_of_target):
            for part in range(width // 128):
                dealt_ref[target, place * rows:(place + 1) * rows, part * 128:(part + 1) * 128] = pieces_ref[
                    tile, part * rows:(part + 1) * rows, :
                ]
    total = jnp.zeros((TAIL, 128), F32)
    for column in range(columns):
        total = total + pieces_ref[column, high - TAIL:, :].astype(F32)
    trace_ref[...] = jnp.broadcast_to(jnp.sum(total, axis=0, keepdims=True), (8, 128))


def eliminate(work_ref, first, micro):
    lanes = work_ref.shape[1]
    groups = micro // 8
    rows = [[work_ref[first + 8 * g:first + 8 * g + 8, 128 * w:128 * w + 128] for w in range(lanes // 128)] for g in range(groups)]
    part, lane = first // 128, first % 128
    for begin in range(0, micro, STRIP):
        columns = {
            k: {g: jnp.broadcast_to(rows[g][part][:, lane + k:lane + k + 1], (8, 128)) for g in range(begin // 8, groups)}
            for k in range(begin, begin + STRIP)
        }
        for j in range(begin, begin + STRIP):
            group, line = j // 8, j % 8

            def spread(value):
                return jnp.broadcast_to(value[line:line + 1, :], (8, 128))

            pivot = spread(columns[j][group])
            inverse = 1.0 / pivot
            scale = lax.rsqrt(pivot)
            live = range((j + 1) // 8, groups)
            multiplier = {g: columns[j][g] * inverse for g in live}
            for k in range(j + 1, begin + STRIP):
                entry = spread(columns[k][group])
                for g in live:
                    columns[k][g] = columns[k][g] - multiplier[g] * entry
            for w in range(lanes // 128):
                entry = spread(rows[group][w])
                work_ref[first + j:first + j + 1, 128 * w:128 * w + 128] = (entry * scale)[0:1, :]
                for g in live:
                    rows[g][w] = rows[g][w] - multiplier[g] * entry


def factor_block(work_ref, block, micro):
    for first in range(0, block, micro):
        eliminate(work_ref, first, micro)
        after = first + micro
        if after < block:
            panel = work_ref[first:after, :]
            work_ref[after:, :] = work_ref[after:, :] - exact_dot(panel[:, after:block], panel, ((0,), (0,)))


def identity(size):
    return jnp.where(
        lax.broadcasted_iota(jnp.int32, (size, size), 0) == lax.broadcasted_iota(jnp.int32, (size, size), 1), 1.0, 0.0
    ).astype(F32)


def factor_panel(panel_ref, work_ref, order):
    for start in range(0, order, BLOCK):
        stop = start + BLOCK
        work_ref[:, 0:BLOCK] = panel_ref[start:stop, start:stop]
        work_ref[:, BLOCK:] = identity(BLOCK)
        factor_block(work_ref, BLOCK, MICRO)
        panel_ref[start:stop, start:stop] = work_ref[:, 0:BLOCK]
        done = exact_dot(work_ref[:, BLOCK:], panel_ref[start:stop, stop:], ((1,), (0,)))
        panel_ref[start:stop, stop:] = done
        if stop < order:
            panel_ref[stop:order, stop:] = panel_ref[stop:order, stop:] - exact_dot(done[:, 0:order - stop], done, ((0,), (0,)))


def coefficients(number_ref, over_ref, trace_ref, taps):
    shrinkage = number_ref[0].astype(F32) / over_ref[0].astype(F32)
    return 1.0 - shrinkage, shrinkage * trace_ref[0:1, 0:1] / taps


def panel_kernel(taps, number_ref, over_ref, trace_ref, scaled_ref, below_ref, diagonal_ref, panel_ref, work_ref):
    width = scaled_ref.shape[1]

    @pl.when(lax.axis_index("col") == 0)
    def _():
        keep, level = coefficients(number_ref, over_ref, trace_ref, taps)
        own = scaled_ref[...]
        panel_ref[:, 0:width] = (keep / level) * dot(own, own, ((0,), (0,))) + identity(width)
        panel_ref[:, width:] = jnp.transpose(own.astype(F32))
        factor_panel(panel_ref, work_ref, width)
        root = jnp.sqrt(level)
        below_ref[...] = jnp.transpose(panel_ref[:, width:]) * (keep / root)
        line = lax.broadcasted_iota(jnp.int32, (width, width), 0)
        lane = lax.broadcasted_iota(jnp.int32, (width, width), 1)
        diagonal_ref[...] = jnp.transpose(jnp.where(line <= lane, panel_ref[:, 0:width], 0.0)) * root


def tiles_kernel(taps, number_ref, over_ref, trace_ref, scaled_ref, below_ref, diagonal_ref, dealt_ref, out_ref, panel_ref, work_ref):
    sources, _, width = dealt_ref.shape
    samples = scaled_ref.shape[0]
    rows = samples // sources
    positions = out_ref.shape[0]
    row_index, col_index = lax.axis_index("row"), lax.axis_index("col")
    keep, level = coefficients(number_ref, over_ref, trace_ref, taps)

    def finish(right):
        right_high, right_low = split(right)
        for position in range(positions):
            tile = dealt_ref[:, (position + 1) * rows:(position + 2) * rows, :].reshape(samples, width)
            out_ref[position] = dot(tile, right_high, ((0,), (0,))) + dot(tile, right_low, ((0,), (0,)))

    @pl.when(col_index == 0)
    def _():
        finish(below_ref[...])

    @pl.when(col_index > 0)
    def _():
        first_tile = dealt_ref[:, 0:rows, :].reshape(samples, width)
        panel_ref[:, 0:samples] = (keep / level) * dot(first_tile, first_tile, ((1,), (1,))) + identity(samples)
        panel_ref[:, samples:] = identity(samples)
        factor_panel(panel_ref, work_ref, samples)
        inverse_factor = panel_ref[:, samples:]
        high, low = split(keep * exact_dot(inverse_factor, inverse_factor, ((0,), (0,))))
        own = scaled_ref[...]
        finish(dot(high, own, ((1,), (0,))) + dot(low, own, ((1,), (0,))))
        for position in range(positions):
            @pl.when(position * sources + row_index == col_index)
            def _():
                out_ref[position] = out_ref[position] + level * identity(width)

    @pl.when((row_index == 0) & (col_index > 0))
    def _():
        out_ref[0] = jnp.zeros((width, width), F32)

    @pl.when((row_index == 0) & (col_index == 0))
    def _():
        out_ref[0] = diagonal_ref[...]


def limit(mebibytes):
    return pltpu.CompilerParams(vmem_limit_bytes=mebibytes * 2**20)


def copies(samples, count):
    return pl.pallas_call(
        copies_kernel,
        out_shape=jax.ShapeDtypeStruct((count, *samples.shape), BF16),
        in_specs=[VMEM],
        out_specs=VMEM,
        compiler_params=limit(8),
    )(samples)


def scale(counts, gathered, columns):
    count, rows, width = gathered.shape
    return pl.pallas_call(
        scale_kernel,
        out_shape=(
            jax.ShapeDtypeStruct((count * rows, width), BF16),
            jax.ShapeDtypeStruct((columns, rows * width // 128 + TAIL, 128), BF16),
        ),
        in_specs=[VMEM, VMEM],
        out_specs=(VMEM, VMEM),
        compiler_params=limit(16),
    )(counts[None, :], gathered)


def deal(pieces, rows, width, targets):
    columns = pieces.shape[0]
    return pl.pallas_call(
        deal_kernel,
        out_shape=(
            jax.ShapeDtypeStruct((targets, (1 + columns // targets) * rows, width), BF16),
            jax.ShapeDtypeStruct((8, 128), F32),
        ),
        in_specs=[VMEM],
        out_specs=(VMEM, VMEM),
        compiler_params=limit(16),
    )(pieces)


def panel(number, over, trace, scaled, taps):
    samples, width = scaled.shape
    return pl.pallas_call(
        functools.partial(panel_kernel, taps),
        out_shape=(
            jax.ShapeDtypeStruct((samples, width), F32),
            jax.ShapeDtypeStruct((width, width), F32),
        ),
        in_specs=[SMEM, SMEM, VMEM, VMEM],
        out_specs=(VMEM, VMEM),
        scratch_shapes=[
            pltpu.VMEM((width, width + samples), F32),
            pltpu.VMEM((BLOCK, 2 * BLOCK), F32),
        ],
        compiler_params=limit(32),
        cost_estimate=pl.CostEstimate(flops=20 * 10**9, bytes_accessed=2 * 2**20, transcendentals=0),
    )(number, over, trace, scaled)


def tiles(number, over, trace, scaled, below, diagonal, dealt, taps):
    samples, width = scaled.shape
    positions = dealt.shape[1] * dealt.shape[0] // samples - 1
    return pl.pallas_call(
        functools.partial(tiles_kernel, taps),
        out_shape=jax.ShapeDtypeStruct((positions, width, width), F32),
        in_specs=[SMEM, SMEM] + [VMEM] * 5,
        out_specs=VMEM,
        scratch_shapes=[
            pltpu.VMEM((samples, 2 * samples), F32),
            pltpu.VMEM((BLOCK, 2 * BLOCK), F32),
        ],
        compiler_params=limit(32),
    )(number, over, trace, scaled, below, diagonal, dealt)


def per_device(samples, counts, shrink_num, shrink_den):
    rows_count = lax.axis_size("row")
    cols_count = lax.axis_size("col")
    rows, width = samples.shape
    taps = width * cols_count
    gathered = lax.all_to_all(copies(samples, rows_count), "row", 0, 0)
    scaled, pieces = scale(counts, gathered, cols_count)
    exchanged = lax.all_to_all(pieces, "col", 0, 0)
    dealt, trace = deal(exchanged, rows, width, rows_count)
    dealt = lax.all_to_all(dealt, "row", 0, 0)
    below, diagonal = panel(shrink_num, shrink_den, trace, scaled, taps)
    return tiles(shrink_num, shrink_den, trace, scaled, below, diagonal, dealt, taps)


def solution(mesh):
    in_specs = (P("row", "col"), P(), P(), P())
    out_specs = P(None, "row", "col")
    return jax.shard_map(
        per_device, mesh=mesh, in_specs=in_specs, out_specs=out_specs, check_vma=False
    )
```

```python
import functools

import jax
import jax.numpy as jnp
from jax import lax
from jax.experimental import pallas as pl
from jax.experimental.pallas import tpu as pltpu
from jax.sharding import PartitionSpec as P

BLOCK = 128
MICRO = 32
STRIP = 16
TAIL = 8
COARSE = 4
F32 = jnp.float32
BF16 = jnp.bfloat16
VMEM = pl.BlockSpec(memory_space=pltpu.VMEM)
SMEM = pl.BlockSpec(memory_space=pltpu.SMEM)


def dot(left, right, dims, precision=None):
    return lax.dot_general(
        left, right, ((dims[0], dims[1]), ((), ())),
        precision=precision, preferred_element_type=F32,
    )


def split(value):
    high = value.astype(BF16)
    return high, (value - high.astype(F32)).astype(BF16)


def thirds(value):
    high, rest = value.astype(BF16), value
    rest = rest - high.astype(F32)
    middle = rest.astype(BF16)
    return high, middle, (rest - middle.astype(F32)).astype(BF16)


def stack(parts, order, axis):
    return jnp.concatenate([parts[which] for which in order], axis=axis)


LEFT, RIGHT = (0, 0, 1, 0, 1, 2), (0, 1, 0, 2, 1, 0)


def gram(value, first, last):
    parts = thirds(value)
    left = stack([part[:, first:last] for part in parts], LEFT, 0)
    return dot(left, stack(parts, RIGHT, 0), ((0,), (0,)))


def product(left, right):
    return dot(stack(thirds(left), LEFT, 1), stack(thirds(right), RIGHT, 0), ((1,), (0,)))


def copies_kernel(counts_ref, samples_ref, copies_ref, held_ref):
    held_ref[...] = counts_ref[...]
    for target in range(copies_ref.shape[0]):
        copies_ref[target] = samples_ref[...]


def scale_kernel(counts_ref, samples_ref, scaled_ref, pieces_ref):
    count, rows, width = samples_ref.shape
    number = count * rows
    counts = counts_ref[...].astype(F32)
    weights = jnp.broadcast_to(counts / jnp.sum(counts), (8, number))
    column = jnp.transpose(weights)[:, 0:1]
    values = samples_ref[...].reshape(number, width).astype(F32)
    mean = jnp.sum(column * values, axis=0, keepdims=True)
    scaled = (jnp.sqrt(column) * (values - mean)).astype(BF16)
    scaled_ref[...] = scaled
    share = jnp.sum(jnp.square(scaled.astype(F32)), axis=0, keepdims=True)
    share = jnp.broadcast_to(jnp.sum(share, axis=1, keepdims=True), (TAIL, 128))
    high, middle = split(share)
    low = (share - high.astype(F32) - middle.astype(F32)).astype(BF16)
    line = lax.broadcasted_iota(jnp.int32, (TAIL, 128), 0)
    tail = jnp.where(line == 0, high.astype(F32), 0.0)
    tail = jnp.where(line == 1, middle.astype(F32), tail)
    tail = jnp.where(line == 2, low.astype(F32), tail).astype(BF16)
    first = pl.multiple_of(lax.axis_index("row") * rows, rows)
    own = scaled_ref[pl.ds(first, rows), :]
    body = pieces_ref.shape[1] - TAIL
    for target in range(pieces_ref.shape[0]):
        for part in range(width // 128):
            pieces_ref[target, part * rows:(part + 1) * rows, :] = own[:, part * 128:(part + 1) * 128]
        pieces_ref[target, body:, :] = tail


def deal_kernel(pieces_ref, dealt_ref, trace_ref):
    columns, high, _ = pieces_ref.shape
    targets, dealt_rows, width = dealt_ref.shape
    positions = columns // targets
    rows = dealt_rows // (1 + positions)
    for target in range(targets):
        tiles_of_target = [0] + [position * targets + target for position in range(positions)]
        for place, tile in enumerate(tiles_of_target):
            for part in range(width // 128):
                dealt_ref[target, place * rows:(place + 1) * rows, part * 128:(part + 1) * 128] = pieces_ref[
                    tile, part * rows:(part + 1) * rows, :
                ]
    total = jnp.zeros((TAIL, 128), F32)
    for column in range(columns):
        total = total + pieces_ref[column, high - TAIL:, :].astype(F32)
    trace_ref[...] = jnp.broadcast_to(jnp.sum(total, axis=0, keepdims=True), (8, 128))


def eliminate(work_ref, first, micro):
    lanes = work_ref.shape[1]
    groups = micro // 8
    rows = [[work_ref[first + 8 * g:first + 8 * g + 8, 128 * w:128 * w + 128] for w in range(lanes // 128)] for g in range(groups)]
    part, lane = first // 128, first % 128
    for begin in range(0, micro, STRIP):
        columns = {
            k: {g: jnp.broadcast_to(rows[g][part][:, lane + k:lane + k + 1], (8, 128)) for g in range(begin // 8, groups)}
            for k in range(begin, begin + STRIP)
        }
        for j in range(begin, begin + STRIP):
            group, line = j // 8, j % 8

            def spread(value):
                return jnp.broadcast_to(value[line:line + 1, :], (8, 128))

            pivot = spread(columns[j][group])
            inverse = 1.0 / pivot
            scale = lax.rsqrt(pivot)
            live = range((j + 1) // 8, groups)
            multiplier = {g: columns[j][g] * inverse for g in live}
            for k in range(j + 1, begin + STRIP):
                entry = spread(columns[k][group])
                for g in live:
                    columns[k][g] = columns[k][g] - multiplier[g] * entry
            for w in range(lanes // 128):
                entry = spread(rows[group][w])
                work_ref[first + j:first + j + 1, 128 * w:128 * w + 128] = (entry * scale)[0:1, :]
                for g in live:
                    rows[g][w] = rows[g][w] - multiplier[g] * entry


def factor_block(work_ref, block, micro):
    for first in range(0, block, micro):
        eliminate(work_ref, first, micro)
        after = first + micro
        if after < block:
            panel = work_ref[first:after, :]
            work_ref[after:, :] = work_ref[after:, :] - gram(panel, after, block)


def identity(size):
    return jnp.where(
        lax.broadcasted_iota(jnp.int32, (size, size), 0) == lax.broadcasted_iota(jnp.int32, (size, size), 1), 1.0, 0.0
    ).astype(F32)


def factor_panel(panel_ref, work_ref, order):
    for start in range(0, order, BLOCK):
        stop = start + BLOCK
        work_ref[:, 0:BLOCK] = panel_ref[start:stop, start:stop]
        work_ref[:, BLOCK:] = identity(BLOCK)
        factor_block(work_ref, BLOCK, MICRO)
        panel_ref[start:stop, start:stop] = work_ref[:, 0:BLOCK]
        done = product(work_ref[:, BLOCK:], panel_ref[start:stop, stop:])
        panel_ref[start:stop, stop:] = done
        if stop < order:
            panel_ref[stop:order, stop:] = panel_ref[stop:order, stop:] - gram(done, 0, order - stop)


def coefficients(number_ref, over_ref, trace_ref, taps):
    shrinkage = number_ref[0].astype(F32) / over_ref[0].astype(F32)
    return 1.0 - shrinkage, shrinkage * trace_ref[0:1, 0:1] / taps


def panel_kernel(taps, number_ref, over_ref, trace_ref, scaled_ref, below_ref, diagonal_ref, panel_ref, work_ref):
    width = scaled_ref.shape[1]

    @pl.when(lax.axis_index("col") == 0)
    def _():
        keep, level = coefficients(number_ref, over_ref, trace_ref, taps)
        own = scaled_ref[...]
        panel_ref[:, 0:width] = (keep / level) * dot(own, own, ((0,), (0,))) + identity(width)
        panel_ref[:, width:] = jnp.transpose(own.astype(F32))
        factor_panel(panel_ref, work_ref, width)
        root = jnp.sqrt(level)
        below_ref[...] = jnp.transpose(panel_ref[:, width:]) * (keep / root)
        line = lax.broadcasted_iota(jnp.int32, (width, width), 0)
        lane = lax.broadcasted_iota(jnp.int32, (width, width), 1)
        diagonal_ref[...] = jnp.transpose(jnp.where(line <= lane, panel_ref[:, 0:width], 0.0)) * root


def tiles_kernel(taps, number_ref, over_ref, trace_ref, scaled_ref, below_ref, diagonal_ref, dealt_ref, out_ref, panel_ref, work_ref):
    sources, _, width = dealt_ref.shape
    samples = scaled_ref.shape[0]
    rows = samples // sources
    positions = out_ref.shape[0]
    row_index, col_index = lax.axis_index("row"), lax.axis_index("col")
    keep, level = coefficients(number_ref, over_ref, trace_ref, taps)

    def finish(right):
        both = jnp.concatenate(split(right), axis=0)
        for position in range(positions):
            tile = dealt_ref[:, (position + 1) * rows:(position + 2) * rows, :].reshape(samples, width)
            out_ref[position] = dot(jnp.concatenate([tile, tile], axis=0), both, ((0,), (0,)))

    @pl.when(col_index == 0)
    def _():
        finish(below_ref[...])

    @pl.when(col_index > 0)
    def _():
        first_tile = dealt_ref[:, 0:rows, :].reshape(samples, width)
        panel_ref[:, 0:samples] = (keep / level) * dot(first_tile, first_tile, ((1,), (1,))) + identity(samples)
        panel_ref[:, samples:] = identity(samples)
        factor_panel(panel_ref, work_ref, samples)
        inverse_factor = panel_ref[:, samples:]
        parts = jnp.concatenate(split(keep * gram(inverse_factor, 0, samples)), axis=1)
        own = scaled_ref[...]
        finish(dot(parts, jnp.concatenate([own, own], axis=0), ((1,), (0,))))
        for position in range(positions):
            @pl.when(position * sources + row_index == col_index)
            def _():
                out_ref[position] = out_ref[position] + level * identity(width)

    @pl.when((row_index == 0) & (col_index > 0))
    def _():
        out_ref[0] = jnp.zeros((width, width), F32)

    @pl.when((row_index == 0) & (col_index == 0))
    def _():
        out_ref[0] = diagonal_ref[...]


def limit(mebibytes):
    return pltpu.CompilerParams(vmem_limit_bytes=mebibytes * 2**20)


def copies(counts, samples, count):
    return pl.pallas_call(
        copies_kernel,
        out_shape=(
            jax.ShapeDtypeStruct((count, *samples.shape), BF16),
            jax.ShapeDtypeStruct((1, *counts.shape), counts.dtype),
        ),
        in_specs=[VMEM, VMEM],
        out_specs=(VMEM, VMEM),
        compiler_params=limit(8),
    )(counts[None, :], samples)


def scale(counts, gathered, columns):
    count, rows, width = gathered.shape
    return pl.pallas_call(
        scale_kernel,
        out_shape=(
            jax.ShapeDtypeStruct((count * rows, width), BF16),
            jax.ShapeDtypeStruct((columns, rows * width // 128 + TAIL, 128), BF16),
        ),
        in_specs=[VMEM, VMEM],
        out_specs=(VMEM, VMEM),
        compiler_params=limit(16),
    )(counts, gathered)


def deal(pieces, rows, width, targets):
    columns = pieces.shape[0]
    return pl.pallas_call(
        deal_kernel,
        out_shape=(
            jax.ShapeDtypeStruct((targets, (1 + columns // targets) * rows, width), BF16),
            jax.ShapeDtypeStruct((8, 128), F32),
        ),
        in_specs=[VMEM],
        out_specs=(VMEM, VMEM),
        compiler_params=limit(16),
    )(pieces)


def panel(number, over, trace, scaled, taps):
    samples, width = scaled.shape
    return pl.pallas_call(
        functools.partial(panel_kernel, taps),
        out_shape=(
            jax.ShapeDtypeStruct((samples, width), F32),
            jax.ShapeDtypeStruct((width, width), F32),
        ),
        in_specs=[SMEM, SMEM, VMEM, VMEM],
        out_specs=(VMEM, VMEM),
        scratch_shapes=[
            pltpu.VMEM((width, width + samples), F32),
            pltpu.VMEM((BLOCK, 2 * BLOCK), F32),
        ],
        compiler_params=limit(32),
        cost_estimate=pl.CostEstimate(flops=20 * 10**9, bytes_accessed=2 * 2**20, transcendentals=0),
    )(number, over, trace, scaled)


def tiles(number, over, trace, scaled, below, diagonal, dealt, taps):
    samples, width = scaled.shape
    positions = dealt.shape[1] * dealt.shape[0] // samples - 1
    return pl.pallas_call(
        functools.partial(tiles_kernel, taps),
        out_shape=jax.ShapeDtypeStruct((positions, width, width), F32),
        in_specs=[SMEM, SMEM] + [VMEM] * 5,
        out_specs=VMEM,
        scratch_shapes=[
            pltpu.VMEM((samples, 2 * samples), F32),
            pltpu.VMEM((BLOCK, 2 * BLOCK), F32),
        ],
        compiler_params=limit(32),
    )(number, over, trace, scaled, below, diagonal, dealt)


def near_groups(rows_count, cols_count):
    fine = cols_count // COARSE
    groups = []
    for column in range(cols_count):
        mirrored = (COARSE - 1 - column // fine) * fine + column % fine
        groups.append(
            [row * cols_count + (column if 2 * row < rows_count else mirrored) for row in range(rows_count)]
        )
    return groups


def per_device(samples, counts, shrink_num, shrink_den):
    rows_count = lax.axis_size("row")
    cols_count = lax.axis_size("col")
    rows, width = samples.shape
    taps = width * cols_count
    own, counts = copies(counts, samples, rows_count)
    gathered = lax.all_to_all(own, "row", 0, 0)
    scaled, pieces = scale(counts, gathered, cols_count)
    exchanged = lax.all_to_all(pieces, "col", 0, 0)
    dealt, trace = deal(exchanged, rows, width, rows_count)
    dealt = lax.all_to_all(dealt, ("row", "col"), 0, 0, axis_index_groups=near_groups(rows_count, cols_count))
    below, diagonal = panel(shrink_num, shrink_den, trace, scaled, taps)
    return tiles(shrink_num, shrink_den, trace, scaled, below, diagonal, dealt, taps)


def solution(mesh):
    in_specs = (P("row", "col"), P(), P(), P())
    out_specs = P(None, "row", "col")
    return jax.shard_map(
        per_device, mesh=mesh, in_specs=in_specs, out_specs=out_specs, check_vma=False
    )
```

```python
import functools

import jax
import jax.numpy as jnp
from jax import lax
from jax.experimental import pallas as pl
from jax.experimental.pallas import tpu as pltpu
from jax.sharding import PartitionSpec as P

BLOCK = 128
MICRO = 32
STRIP = 16
TAIL = 8
COARSE = 4
F32 = jnp.float32
BF16 = jnp.bfloat16
VMEM = pl.BlockSpec(memory_space=pltpu.VMEM)
SMEM = pl.BlockSpec(memory_space=pltpu.SMEM)


def dot(left, right, dims, precision=None):
    return lax.dot_general(
        left, right, ((dims[0], dims[1]), ((), ())),
        precision=precision, preferred_element_type=F32,
    )


def split(value):
    high = value.astype(BF16)
    return high, (value - high.astype(F32)).astype(BF16)


def thirds(value):
    high, rest = value.astype(BF16), value
    rest = rest - high.astype(F32)
    middle = rest.astype(BF16)
    return high, middle, (rest - middle.astype(F32)).astype(BF16)


def stack(parts, order, axis):
    return jnp.concatenate([parts[which] for which in order], axis=axis)


LEFT, RIGHT = (0, 0, 1, 0, 1, 2), (0, 1, 0, 2, 1, 0)


def gram(value, first, last):
    parts = thirds(value)
    left = stack([part[:, first:last] for part in parts], LEFT, 0)
    return dot(left, stack(parts, RIGHT, 0), ((0,), (0,)))


def product(left, right):
    return dot(stack(thirds(left), LEFT, 1), stack(thirds(right), RIGHT, 0), ((1,), (0,)))


def copies_kernel(counts_ref, samples_ref, copies_ref, held_ref):
    held_ref[...] = counts_ref[...]
    for target in range(copies_ref.shape[0]):
        copies_ref[target] = samples_ref[...]


def columns_of(counts):
    counts = counts.astype(F32)
    weights = jnp.broadcast_to(counts / jnp.sum(counts), (128, counts.shape[1]))
    return jnp.transpose(weights)


def scale_tile(weights, roots, samples):
    repeats = samples.shape[1] // 128
    values = samples.astype(F32)
    mean = jnp.sum(jnp.concatenate([weights] * repeats, axis=1) * values, axis=0, keepdims=True)
    return (jnp.concatenate([roots] * repeats, axis=1) * (values - mean)).astype(BF16)


def scale_kernel(counts_ref, samples_ref, helped_ref, helped_too_ref, scaled_ref, pieces_ref):
    count, rows, width = samples_ref.shape
    weights = columns_of(counts_ref[...])
    scaled = scale_tile(weights, jnp.sqrt(weights), samples_ref[...].reshape(count * rows, width))
    scaled_ref[...] = scaled
    share = jnp.sum(jnp.square(scaled.astype(F32)), axis=0, keepdims=True)
    share = jnp.broadcast_to(jnp.sum(share, axis=1, keepdims=True), (TAIL, 128))
    high, middle = split(share)
    low = (share - high.astype(F32) - middle.astype(F32)).astype(BF16)
    line = lax.broadcasted_iota(jnp.int32, (TAIL, 128), 0)
    tail = jnp.where(line == 0, high.astype(F32), 0.0)
    tail = jnp.where(line == 1, middle.astype(F32), tail)
    tail = jnp.where(line == 2, low.astype(F32), tail).astype(BF16)
    half, place = lax.axis_index("row") // (count // 2), lax.rem(lax.axis_index("row"), count // 2)
    column = lax.axis_index("col")
    fine = pieces_ref.shape[0] // COARSE
    own = lax.rem(column // fine, 2) == half
    own = (column == 0) | (own & ((half == 0) | (column != fine)))
    helped = helped_ref[...].astype(F32) + helped_too_ref[...].astype(F32)
    sent = jnp.where(own, samples_ref[2 * place].astype(F32), helped).astype(BF16)
    body = pieces_ref.shape[1] - TAIL
    for target in range(pieces_ref.shape[0]):
        for part in range(width // 128):
            pieces_ref[target, part * rows:(part + 1) * rows, :] = sent[:, part * 128:(part + 1) * 128]
        pieces_ref[target, body:, :] = tail


def deal_kernel(pieces_ref, dealt_ref, trace_ref):
    columns, high, _ = pieces_ref.shape
    targets, dealt_rows, width = dealt_ref.shape
    fine = columns // COARSE
    rows = dealt_rows // 6
    half = lax.axis_index("row") // targets
    first, second = half * fine, (1 - half) * fine
    for target in range(targets):
        sources = (0, fine, first + target, second + target, first + 2 * fine + target, second + 2 * fine + target)
        for place, source in enumerate(sources):
            for part in range(width // 128):
                dealt_ref[target, place * rows:(place + 1) * rows, part * 128:(part + 1) * 128] = pieces_ref[
                    source, part * rows:(part + 1) * rows, :
                ]
    total = jnp.zeros((TAIL, 128), F32)
    for column in range(columns):
        total = total + pieces_ref[column, high - TAIL:, :].astype(F32)
    trace_ref[...] = jnp.broadcast_to(jnp.sum(total, axis=0, keepdims=True), (8, 128))


def eliminate(work_ref, first, micro):
    lanes = work_ref.shape[1]
    groups = micro // 8
    rows = [[work_ref[first + 8 * g:first + 8 * g + 8, 128 * w:128 * w + 128] for w in range(lanes // 128)] for g in range(groups)]
    part, lane = first // 128, first % 128
    for begin in range(0, micro, STRIP):
        columns = {
            k: {g: jnp.broadcast_to(rows[g][part][:, lane + k:lane + k + 1], (8, 128)) for g in range(begin // 8, groups)}
            for k in range(begin, begin + STRIP)
        }
        for j in range(begin, begin + STRIP):
            group, line = j // 8, j % 8

            def spread(value):
                return jnp.broadcast_to(value[line:line + 1, :], (8, 128))

            pivot = spread(columns[j][group])
            inverse = 1.0 / pivot
            scale = lax.rsqrt(pivot)
            live = range((j + 1) // 8, groups)
            multiplier = {g: columns[j][g] * inverse for g in live}
            for k in range(j + 1, begin + STRIP):
                entry = spread(columns[k][group])
                for g in live:
                    columns[k][g] = columns[k][g] - multiplier[g] * entry
            for w in range(lanes // 128):
                entry = spread(rows[group][w])
                work_ref[first + j:first + j + 1, 128 * w:128 * w + 128] = (entry * scale)[0:1, :]
                for g in live:
                    rows[g][w] = rows[g][w] - multiplier[g] * entry


def factor_block(work_ref, block, micro):
    for first in range(0, block, micro):
        eliminate(work_ref, first, micro)
        after = first + micro
        if after < block:
            panel = work_ref[first:after, :]
            work_ref[after:, :] = work_ref[after:, :] - gram(panel, after, block)


def identity(size):
    return jnp.where(
        lax.broadcasted_iota(jnp.int32, (size, size), 0) == lax.broadcasted_iota(jnp.int32, (size, size), 1), 1.0, 0.0
    ).astype(F32)


def factor_panel(panel_ref, work_ref, order):
    for start in range(0, order, BLOCK):
        stop = start + BLOCK
        work_ref[:, 0:BLOCK] = panel_ref[start:stop, start:stop]
        work_ref[:, BLOCK:] = identity(BLOCK)
        factor_block(work_ref, BLOCK, MICRO)
        panel_ref[start:stop, start:stop] = work_ref[:, 0:BLOCK]
        done = product(work_ref[:, BLOCK:], panel_ref[start:stop, stop:])
        panel_ref[start:stop, stop:] = done
        if stop < order:
            panel_ref[stop:order, stop:] = panel_ref[stop:order, stop:] - gram(done, 0, order - stop)


def coefficients(number_ref, over_ref, trace_ref, taps):
    shrinkage = number_ref[0].astype(F32) / over_ref[0].astype(F32)
    return 1.0 - shrinkage, shrinkage * trace_ref[0:1, 0:1] / taps


def panel_kernel(taps, number_ref, over_ref, trace_ref, scaled_ref, below_ref, diagonal_ref, panel_ref, work_ref):
    width = scaled_ref.shape[1]

    @pl.when(lax.axis_index("col") == 0)
    def _():
        keep, level = coefficients(number_ref, over_ref, trace_ref, taps)
        own = scaled_ref[...]
        panel_ref[:, 0:width] = (keep / level) * dot(own, own, ((0,), (0,))) + identity(width)
        panel_ref[:, width:] = jnp.transpose(own.astype(F32))
        factor_panel(panel_ref, work_ref, width)
        root = jnp.sqrt(level)
        below_ref[...] = jnp.transpose(panel_ref[:, width:]) * (keep / root)
        line = lax.broadcasted_iota(jnp.int32, (width, width), 0)
        lane = lax.broadcasted_iota(jnp.int32, (width, width), 1)
        diagonal_ref[...] = jnp.transpose(jnp.where(line <= lane, panel_ref[:, 0:width], 0.0)) * root


def right_kernel(
    taps, number_ref, over_ref, trace_ref, counts_ref, scaled_ref, below_ref, dealt_ref, right_ref, tiles_ref, panel_ref, work_ref
):
    samples, width = scaled_ref.shape
    rows = samples // dealt_ref.shape[0]
    weights = columns_of(counts_ref[...])
    roots = jnp.sqrt(weights)

    def tile(place):
        return scale_tile(weights, roots, dealt_ref[:, place * rows:(place + 1) * rows, :].reshape(samples, width))

    for position in range(tiles_ref.shape[0]):
        tiles_ref[position] = tile(position + 1)

    @pl.when(lax.axis_index("col") == 0)
    def _():
        right_ref[...] = jnp.concatenate(split(below_ref[...]), axis=0)

    @pl.when(lax.axis_index("col") > 0)
    def _():
        keep, level = coefficients(number_ref, over_ref, trace_ref, taps)
        first_tile = tile(0)
        panel_ref[:, 0:samples] = (keep / level) * dot(first_tile, first_tile, ((1,), (1,))) + identity(samples)
        panel_ref[:, samples:] = identity(samples)
        factor_panel(panel_ref, work_ref, samples)
        inverse_factor = panel_ref[:, samples:]
        parts = jnp.concatenate(split(keep * gram(inverse_factor, 0, samples)), axis=1)
        own = scaled_ref[...]
        right_ref[...] = jnp.concatenate(split(dot(parts, jnp.concatenate([own, own], axis=0), ((1,), (0,)))), axis=0)


def finish_kernel(
    taps, number_ref, over_ref, trace_ref, counts_ref, right_ref, tiles_ref, diagonal_ref, eight_ref, even_ref, odd_ref, out_ref,
    held_ref, arrived,
):
    positions, samples, width = tiles_ref.shape
    row_index, col_index = lax.axis_index("row"), lax.axis_index("col")
    rows_count = lax.axis_size("row")

    def fill(position, tile):
        out_ref[position] = dot(jnp.concatenate([tile, tile], axis=0), right_ref[...], ((0,), (0,)))

    for position in range(1, positions):
        fill(position, tiles_ref[position])

    @pl.when((2 * row_index == rows_count))
    def _():
        copies_in = [
            pltpu.make_async_copy(source, held_ref.at[place], arrived.at[place])
            for place, source in enumerate((eight_ref, even_ref, odd_ref))
        ]
        for copy in copies_in:
            copy.start()
        for copy in copies_in:
            copy.wait()
        weights = columns_of(counts_ref[...])
        eight = held_ref[0].astype(F32) + held_ref[1].astype(F32) + held_ref[2].astype(F32)
        fill(0, scale_tile(weights, jnp.sqrt(weights), eight))

    @pl.when((2 * row_index != rows_count) & (row_index > 0))
    def _():
        fill(0, tiles_ref[0])

    @pl.when((row_index == 0) & (col_index > 0))
    def _():
        out_ref[0] = jnp.zeros((width, width), F32)

    @pl.when((row_index == 0) & (col_index == 0))
    def _():
        out_ref[0] = diagonal_ref[...]

    for position in range(positions):
        @pl.when((position * rows_count + row_index == col_index) & (col_index > 0))
        def _():
            _, level = coefficients(number_ref, over_ref, trace_ref, taps)
            out_ref[position] = out_ref[position] + level * identity(width)


def limit(mebibytes):
    return pltpu.CompilerParams(vmem_limit_bytes=mebibytes * 2**20)


def copies(counts, samples, count):
    return pl.pallas_call(
        copies_kernel,
        out_shape=(
            jax.ShapeDtypeStruct((count, *samples.shape), BF16),
            jax.ShapeDtypeStruct((1, *counts.shape), counts.dtype),
        ),
        in_specs=[VMEM, VMEM],
        out_specs=(VMEM, VMEM),
        compiler_params=limit(8),
    )(counts[None, :], samples)


def scale(counts, gathered, helped, helped_too, columns):
    count, rows, width = gathered.shape
    return pl.pallas_call(
        scale_kernel,
        out_shape=(
            jax.ShapeDtypeStruct((count * rows, width), BF16),
            jax.ShapeDtypeStruct((columns, rows * width // 128 + TAIL, 128), BF16),
        ),
        in_specs=[VMEM] * 4,
        out_specs=(VMEM, VMEM),
        compiler_params=limit(16),
    )(counts, gathered, helped, helped_too)


def deal(pieces, rows, width, targets):
    return pl.pallas_call(
        deal_kernel,
        out_shape=(
            jax.ShapeDtypeStruct((targets, 6 * rows, width), BF16),
            jax.ShapeDtypeStruct((8, 128), F32),
        ),
        in_specs=[VMEM],
        out_specs=(VMEM, VMEM),
        compiler_params=limit(16),
    )(pieces)


def hold_kernel(_, value_ref, held_ref):
    count, rows, _ = value_ref.shape
    held_ref[...] = value_ref[...].reshape(count * rows, -1)


def hold(value, after):
    count, rows, width = value.shape
    return pl.pallas_call(
        hold_kernel,
        out_shape=jax.ShapeDtypeStruct((count * rows, width), BF16),
        in_specs=[pl.BlockSpec(memory_space=pl.ANY), VMEM],
        out_specs=VMEM,
        compiler_params=limit(8),
    )(after, value)


def panel(number, over, trace, scaled, taps):
    samples, width = scaled.shape
    return pl.pallas_call(
        functools.partial(panel_kernel, taps),
        out_shape=(
            jax.ShapeDtypeStruct((samples, width), F32),
            jax.ShapeDtypeStruct((width, width), F32),
        ),
        in_specs=[SMEM, SMEM, VMEM, VMEM],
        out_specs=(VMEM, VMEM),
        scratch_shapes=[
            pltpu.VMEM((width, width + samples), F32),
            pltpu.VMEM((BLOCK, 2 * BLOCK), F32),
        ],
        compiler_params=limit(32),
        cost_estimate=pl.CostEstimate(flops=20 * 10**9, bytes_accessed=2 * 2**20, transcendentals=0),
    )(number, over, trace, scaled)


def right_factor(number, over, trace, counts, scaled, below, dealt, taps):
    samples, width = scaled.shape
    return pl.pallas_call(
        functools.partial(right_kernel, taps),
        out_shape=(
            jax.ShapeDtypeStruct((2 * samples, width), BF16),
            jax.ShapeDtypeStruct((2, samples, width), BF16),
        ),
        in_specs=[SMEM, SMEM] + [VMEM] * 5,
        out_specs=(VMEM, VMEM),
        scratch_shapes=[
            pltpu.VMEM((samples, 2 * samples), F32),
            pltpu.VMEM((BLOCK, 2 * BLOCK), F32),
        ],
        compiler_params=limit(32),
        cost_estimate=pl.CostEstimate(flops=10**10, bytes_accessed=2 * 2**20, transcendentals=0),
    )(number, over, trace, counts, scaled, below, dealt)


def finish(number, over, trace, counts, right, tiles, diagonal, eights, taps):
    positions, samples, width = tiles.shape
    return pl.pallas_call(
        functools.partial(finish_kernel, taps),
        out_shape=jax.ShapeDtypeStruct((positions, width, width), F32),
        in_specs=[SMEM, SMEM] + [VMEM] * 5 + [pl.BlockSpec(memory_space=pl.ANY)] * 3,
        out_specs=VMEM,
        scratch_shapes=[pltpu.VMEM((3, samples, width), BF16), pltpu.SemaphoreType.DMA((3,))],
        compiler_params=limit(32),
    )(number, over, trace, counts, right, tiles, diagonal, *eights)


def helper_pairs(rows_count, cols_count):
    fine, half_rows = cols_count // COARSE, rows_count // 2
    pairs, too = [], []
    for place in range(half_rows):
        source = (2 * place + 1) * cols_count
        for tile in range(cols_count):
            half = tile // fine % 2
            helper = tile + fine * (1 - 2 * half)
            if tile != fine:
                pairs.append((source + tile, (half * half_rows + place) * cols_count + helper))
        too.append((source, (half_rows + place) * cols_count + fine))
    return pairs, too


def eight_pairs(rows_count, cols_count):
    fine = cols_count // COARSE
    wanted = rows_count // 2 * cols_count
    first = [(fine, wanted)]
    return first, [
        [(row * cols_count + fine, wanted + 2 * row + turn) for row in range(rows_count) if row + turn > 0] for turn in range(2)
    ]


def per_device(samples, counts, shrink_num, shrink_den):
    rows_count = lax.axis_size("row")
    cols_count = lax.axis_size("col")
    rows, width = samples.shape
    taps = width * cols_count
    both = ("row", "col")
    helped, helped_too = (lax.ppermute(samples, both, pairs) for pairs in helper_pairs(rows_count, cols_count))
    own, counts = copies(counts, samples, rows_count)
    gathered = lax.all_to_all(own, "row", 0, 0)
    scaled, pieces = scale(counts, gathered, helped, helped_too, cols_count)
    pairs_first, pairs_late = eight_pairs(rows_count, cols_count)
    eights = [lax.ppermute(gathered.reshape(rows_count * rows, width), both, pairs_first)]
    exchanged = lax.all_to_all(pieces, "col", 0, 0)
    half_rows = rows_count // 2
    dealt, trace = deal(exchanged, rows, width, half_rows)
    halves = [list(range(half_rows)), list(range(half_rows, rows_count))]
    dealt = lax.all_to_all(dealt, "row", 0, 0, axis_index_groups=halves)
    below, diagonal = panel(shrink_num, shrink_den, trace, scaled, taps)
    whole = hold(gathered, below)
    eights += [lax.ppermute(whole, both, pairs) for pairs in pairs_late]
    right, tiles = right_factor(shrink_num, shrink_den, trace, counts, scaled, below, dealt, taps)
    return finish(shrink_num, shrink_den, trace, counts, right, tiles, diagonal, eights, taps)


def solution(mesh):
    in_specs = (P("row", "col"), P(), P(), P())
    out_specs = P(None, "row", "col")
    return jax.shard_map(
        per_device, mesh=mesh, in_specs=in_specs, out_specs=out_specs, check_vma=False
    )
```

```python
import functools

import jax
import jax.numpy as jnp
from jax import lax
from jax.experimental import pallas as pl
from jax.experimental.pallas import tpu as pltpu
from jax.sharding import PartitionSpec as P

BLOCK = 128
MICRO = 32
STRIP = 16
TAIL = 8
COARSE = 4
F32 = jnp.float32
BF16 = jnp.bfloat16
VMEM = pl.BlockSpec(memory_space=pltpu.VMEM)
SMEM = pl.BlockSpec(memory_space=pltpu.SMEM)


def dot(left, right, dims, precision=None):
    return lax.dot_general(
        left, right, ((dims[0], dims[1]), ((), ())),
        precision=precision, preferred_element_type=F32,
    )


def split(value):
    high = value.astype(BF16)
    return high, (value - high.astype(F32)).astype(BF16)


def thirds(value):
    high, rest = value.astype(BF16), value
    rest = rest - high.astype(F32)
    middle = rest.astype(BF16)
    return high, middle, (rest - middle.astype(F32)).astype(BF16)


def stack(parts, order, axis):
    return jnp.concatenate([parts[which] for which in order], axis=axis)


LEFT, RIGHT = (0, 0, 1, 0, 1, 2), (0, 1, 0, 2, 1, 0)


def gram(value, first, last):
    parts = thirds(value)
    left = stack([part[:, first:last] for part in parts], LEFT, 0)
    return dot(left, stack(parts, RIGHT, 0), ((0,), (0,)))


def product(left, right):
    return dot(stack(thirds(left), LEFT, 1), stack(thirds(right), RIGHT, 0), ((1,), (0,)))


def copies_kernel(samples_ref, copies_ref):
    for target in range(copies_ref.shape[0]):
        copies_ref[target] = samples_ref[...]


def columns_of(counts):
    counts = counts.astype(F32)
    weights = jnp.broadcast_to(counts / jnp.sum(counts), (128, counts.shape[1]))
    return jnp.transpose(weights)


def scale_tile(weights, roots, samples):
    repeats = samples.shape[1] // 128
    values = samples.astype(F32)
    mean = jnp.sum(jnp.concatenate([weights] * repeats, axis=1) * values, axis=0, keepdims=True)
    return (jnp.concatenate([roots] * repeats, axis=1) * (values - mean)).astype(BF16)


def weights_kernel(counts_ref, weights_ref):
    weights = columns_of(counts_ref[...])
    weights_ref[0] = weights
    weights_ref[1] = jnp.sqrt(weights)


def scale_kernel(weights_ref, samples_ref, helped_ref, scaled_ref, pieces_ref):
    count, rows, width = samples_ref.shape
    scaled = scale_tile(weights_ref[0], weights_ref[1], samples_ref[...].reshape(count * rows, width))
    scaled_ref[...] = scaled
    share = jnp.sum(jnp.square(scaled.astype(F32)), axis=0, keepdims=True)
    share = jnp.broadcast_to(jnp.sum(share, axis=1, keepdims=True), (TAIL, 128))
    high, middle = split(share)
    low = (share - high.astype(F32) - middle.astype(F32)).astype(BF16)
    line = lax.broadcasted_iota(jnp.int32, (TAIL, 128), 0)
    tail = jnp.where(line == 0, high.astype(F32), 0.0)
    tail = jnp.where(line == 1, middle.astype(F32), tail)
    tail = jnp.where(line == 2, low.astype(F32), tail).astype(BF16)
    row = lax.axis_index("row")
    half = row // (count // 2)
    column = lax.axis_index("col")
    fine = pieces_ref.shape[0] // COARSE
    own = lax.rem(column // fine, 2) == half
    own = (column == 0) | (own & ((half == 0) | (column != fine)))
    other_block = samples_ref[lax.rem(row + count // 2, count)].astype(F32)
    sent = jnp.where(own, other_block, helped_ref[...].astype(F32)).astype(BF16)
    body = pieces_ref.shape[1] - TAIL
    for target in range(pieces_ref.shape[0]):
        for part in range(width // 128):
            pieces_ref[target, part * rows:(part + 1) * rows, :] = sent[:, part * 128:(part + 1) * 128]
        pieces_ref[target, body:, :] = tail


def deal_kernel(pieces_ref, dealt_ref, trace_ref):
    columns, high, _ = pieces_ref.shape
    targets, dealt_rows, width = dealt_ref.shape
    fine = columns // COARSE
    rows = dealt_rows // 6
    half = lax.axis_index("row") // targets
    for target in range(targets):
        sources = ((1 - half) * fine, half * fine, fine + target, target, 3 * fine + target, 2 * fine + target)
        for place, source in enumerate(sources):
            for part in range(width // 128):
                dealt_ref[target, place * rows:(place + 1) * rows, part * 128:(part + 1) * 128] = pieces_ref[
                    source, part * rows:(part + 1) * rows, :
                ]
    total = jnp.zeros((TAIL, 128), F32)
    for column in range(columns):
        total = total + pieces_ref[column, high - TAIL:, :].astype(F32)
    trace_ref[...] = jnp.broadcast_to(jnp.sum(total, axis=0, keepdims=True), (8, 128))


def eliminate(work_ref, first, micro):
    lanes = work_ref.shape[1]
    groups = micro // 8
    rows = [[work_ref[first + 8 * g:first + 8 * g + 8, 128 * w:128 * w + 128] for w in range(lanes // 128)] for g in range(groups)]
    part, lane = first // 128, first % 128
    for begin in range(0, micro, STRIP):
        columns = {
            k: {g: jnp.broadcast_to(rows[g][part][:, lane + k:lane + k + 1], (8, 128)) for g in range(begin // 8, groups)}
            for k in range(begin, begin + STRIP)
        }
        for j in range(begin, begin + STRIP):
            group, line = j // 8, j % 8

            def spread(value):
                return jnp.broadcast_to(value[line:line + 1, :], (8, 128))

            pivot = spread(columns[j][group])
            inverse = 1.0 / pivot
            scale = lax.rsqrt(pivot)
            live = range((j + 1) // 8, groups)
            multiplier = {g: columns[j][g] * inverse for g in live}
            for k in range(j + 1, begin + STRIP):
                entry = spread(columns[k][group])
                for g in live:
                    columns[k][g] = columns[k][g] - multiplier[g] * entry
            for w in range(lanes // 128):
                entry = spread(rows[group][w])
                work_ref[first + j:first + j + 1, 128 * w:128 * w + 128] = (entry * scale)[0:1, :]
                for g in live:
                    rows[g][w] = rows[g][w] - multiplier[g] * entry


def factor_block(work_ref, block, micro):
    for first in range(0, block, micro):
        eliminate(work_ref, first, micro)
        after = first + micro
        if after < block:
            panel = work_ref[first:after, :]
            work_ref[after:, :] = work_ref[after:, :] - gram(panel, after, block)


def identity(size):
    return jnp.where(
        lax.broadcasted_iota(jnp.int32, (size, size), 0) == lax.broadcasted_iota(jnp.int32, (size, size), 1), 1.0, 0.0
    ).astype(F32)


def factor_panel(panel_ref, work_ref, order):
    for start in range(0, order, BLOCK):
        stop = start + BLOCK
        work_ref[:, 0:BLOCK] = panel_ref[start:stop, start:stop]
        work_ref[:, BLOCK:] = identity(BLOCK)
        factor_block(work_ref, BLOCK, MICRO)
        panel_ref[start:stop, start:stop] = work_ref[:, 0:BLOCK]
        done = product(work_ref[:, BLOCK:], panel_ref[start:stop, stop:])
        panel_ref[start:stop, stop:] = done
        if stop < order:
            panel_ref[stop:order, stop:] = panel_ref[stop:order, stop:] - gram(done, 0, order - stop)


def coefficients(number_ref, over_ref, trace_ref, taps):
    shrinkage = number_ref[0].astype(F32) / over_ref[0].astype(F32)
    return 1.0 - shrinkage, shrinkage * trace_ref[0:1, 0:1] / taps


def panel_kernel(taps, number_ref, over_ref, trace_ref, scaled_ref, below_ref, diagonal_ref, panel_ref, work_ref):
    width = scaled_ref.shape[1]

    @pl.when(lax.axis_index("col") > 0)
    def _():
        below_ref[...] = scaled_ref[...].astype(F32)

    @pl.when(lax.axis_index("col") == 0)
    def _():
        keep, level = coefficients(number_ref, over_ref, trace_ref, taps)
        own = scaled_ref[...]
        panel_ref[:, 0:width] = (keep / level) * dot(own, own, ((0,), (0,))) + identity(width)
        panel_ref[:, width:] = jnp.transpose(own.astype(F32))
        factor_panel(panel_ref, work_ref, width)
        root = jnp.sqrt(level)
        below_ref[...] = jnp.transpose(panel_ref[:, width:]) * (keep / root)
        line = lax.broadcasted_iota(jnp.int32, (width, width), 0)
        lane = lax.broadcasted_iota(jnp.int32, (width, width), 1)
        diagonal_ref[...] = jnp.transpose(jnp.where(line <= lane, panel_ref[:, 0:width], 0.0)) * root


def right_kernel(
    taps, number_ref, over_ref, trace_ref, counts_ref, below_ref, dealt_ref, right_ref, tiles_ref, panel_ref, work_ref
):
    samples, width = below_ref.shape
    rows = samples // dealt_ref.shape[0]
    weights = columns_of(counts_ref[...])
    roots = jnp.sqrt(weights)

    def tile(place):
        halves = [
            dealt_ref[:, start:start + rows // 2, :].reshape(samples // 2, width)
            for start in (place * rows, place * rows + rows // 2)
        ]
        return scale_tile(weights, roots, jnp.concatenate(halves, axis=0))

    for position in range(tiles_ref.shape[0]):
        tiles_ref[position] = tile(position + 1)

    @pl.when(lax.axis_index("col") == 0)
    def _():
        right_ref[...] = jnp.concatenate(split(below_ref[...]), axis=0)

    @pl.when(lax.axis_index("col") > 0)
    def _():
        keep, level = coefficients(number_ref, over_ref, trace_ref, taps)
        first_tile = tile(0)
        panel_ref[:, 0:samples] = (keep / level) * dot(first_tile, first_tile, ((1,), (1,))) + identity(samples)
        panel_ref[:, samples:] = identity(samples)
        factor_panel(panel_ref, work_ref, samples)
        inverse_factor = panel_ref[:, samples:]
        parts = jnp.concatenate(split(keep * gram(inverse_factor, 0, samples)), axis=1)
        own = below_ref[...].astype(BF16)
        right_ref[...] = jnp.concatenate(split(dot(parts, jnp.concatenate([own, own], axis=0), ((1,), (0,)))), axis=0)


def finish_kernel(
    taps, number_ref, over_ref, trace_ref, counts_ref, right_ref, tiles_ref, diagonal_ref, eight_ref, even_ref, odd_ref, out_ref,
    held_ref, made_ref, arrived, sent,
):
    positions, samples, width = tiles_ref.shape
    row_index, col_index = lax.axis_index("row"), lax.axis_index("col")
    rows_count = lax.axis_size("row")
    step = width // 2
    moves = []

    def fill(position, start, tile):
        part = tile[:, start:start + step]
        made_ref[position, start:start + step, :] = dot(jnp.concatenate([part, part], axis=0), right_ref[...], ((0,), (0,)))

    def send(position, start):
        @pl.when((position * rows_count + row_index == col_index) & (col_index > 0))
        def _():
            _, level = coefficients(number_ref, over_ref, trace_ref, taps)
            made_ref[position, start:start + step, start:start + step] = (
                made_ref[position, start:start + step, start:start + step] + level * identity(step)
            )
        move = pltpu.make_async_copy(
            made_ref.at[position, pl.ds(start, step)], out_ref.at[position, pl.ds(start, step)], sent.at[position, start // step]
        )
        move.start()
        moves.append(move)

    for start in (0, step):
        fill(1, start, tiles_ref[1])
        send(1, start)

    eighth = 2 * row_index == rows_count

    @pl.when(eighth)
    def _():
        copies_in = [
            pltpu.make_async_copy(source, held_ref.at[place], arrived.at[place])
            for place, source in enumerate((eight_ref, even_ref, odd_ref))
        ]
        for copy in copies_in:
            copy.start()
        for copy in copies_in:
            copy.wait()
        weights = columns_of(counts_ref[...])
        eight = held_ref[0].astype(F32) + held_ref[1].astype(F32) + held_ref[2].astype(F32)
        held_ref[0] = scale_tile(weights, jnp.sqrt(weights), eight)

    for start in (0, step):
        @pl.when(eighth)
        def _():
            fill(0, start, held_ref[0])

        @pl.when(jnp.logical_not(eighth) & (row_index > 0))
        def _():
            fill(0, start, tiles_ref[0])

        @pl.when((row_index == 0) & (col_index > 0))
        def _():
            made_ref[0, start:start + step, :] = jnp.zeros((step, width), F32)

        @pl.when((row_index == 0) & (col_index == 0))
        def _():
            made_ref[0, start:start + step, :] = diagonal_ref[start:start + step, :]

        send(0, start)

    for move in moves:
        move.wait()


def limit(mebibytes):
    return pltpu.CompilerParams(vmem_limit_bytes=mebibytes * 2**20)


def copies(samples, count):
    return pl.pallas_call(
        copies_kernel,
        out_shape=jax.ShapeDtypeStruct((count, *samples.shape), BF16),
        in_specs=[VMEM],
        out_specs=VMEM,
        compiler_params=limit(8),
    )(samples)


def weigh(counts):
    return pl.pallas_call(
        weights_kernel,
        out_shape=jax.ShapeDtypeStruct((2, counts.shape[1], 128), F32),
        in_specs=[VMEM],
        out_specs=VMEM,
        compiler_params=limit(8),
        cost_estimate=pl.CostEstimate(flops=2 * 10**9, bytes_accessed=2 * 2**20, transcendentals=0),
    )(counts)


def scale(weights, gathered, helped, columns):
    count, rows, width = gathered.shape
    return pl.pallas_call(
        scale_kernel,
        out_shape=(
            jax.ShapeDtypeStruct((count * rows, width), BF16),
            jax.ShapeDtypeStruct((columns, rows * width // 128 + TAIL, 128), BF16),
        ),
        in_specs=[VMEM] * 3,
        out_specs=(VMEM, VMEM),
        compiler_params=limit(16),
    )(weights, gathered, helped)


def deal(pieces, rows, width, targets):
    return pl.pallas_call(
        deal_kernel,
        out_shape=(
            jax.ShapeDtypeStruct((targets, 6 * rows, width), BF16),
            jax.ShapeDtypeStruct((8, 128), F32),
        ),
        in_specs=[VMEM],
        out_specs=(VMEM, VMEM),
        compiler_params=limit(16),
    )(pieces)


def hold_kernel(_, value_ref, held_ref):
    count, rows, _ = value_ref.shape
    held_ref[...] = value_ref[...].reshape(count * rows, -1)


def hold(value, after):
    count, rows, width = value.shape
    return pl.pallas_call(
        hold_kernel,
        out_shape=jax.ShapeDtypeStruct((count * rows, width), BF16),
        in_specs=[pl.BlockSpec(memory_space=pl.ANY), VMEM],
        out_specs=VMEM,
        compiler_params=limit(8),
    )(after, value)


def panel(number, over, trace, scaled, taps):
    samples, width = scaled.shape
    return pl.pallas_call(
        functools.partial(panel_kernel, taps),
        out_shape=(
            jax.ShapeDtypeStruct((samples, width), F32),
            jax.ShapeDtypeStruct((width, width), F32),
        ),
        in_specs=[SMEM, SMEM, VMEM, VMEM],
        out_specs=(VMEM, VMEM),
        scratch_shapes=[
            pltpu.VMEM((width, width + samples), F32),
            pltpu.VMEM((BLOCK, 2 * BLOCK), F32),
        ],
        compiler_params=limit(32),
        cost_estimate=pl.CostEstimate(flops=20 * 10**9, bytes_accessed=2 * 2**20, transcendentals=0),
    )(number, over, trace, scaled)


def right_factor(number, over, trace, counts, below, dealt, taps):
    samples, width = below.shape
    return pl.pallas_call(
        functools.partial(right_kernel, taps),
        out_shape=(
            jax.ShapeDtypeStruct((2 * samples, width), BF16),
            jax.ShapeDtypeStruct((2, samples, width), BF16),
        ),
        in_specs=[SMEM, SMEM] + [VMEM] * 4,
        out_specs=(VMEM, VMEM),
        scratch_shapes=[
            pltpu.VMEM((samples, 2 * samples), F32),
            pltpu.VMEM((BLOCK, 2 * BLOCK), F32),
        ],
        compiler_params=limit(32),
        cost_estimate=pl.CostEstimate(flops=10**10, bytes_accessed=2 * 2**20, transcendentals=0),
    )(number, over, trace, counts, below, dealt)


def finish(number, over, trace, counts, right, tiles, diagonal, eights, taps):
    positions, samples, width = tiles.shape
    return pl.pallas_call(
        functools.partial(finish_kernel, taps),
        out_shape=jax.ShapeDtypeStruct((positions, width, width), F32),
        in_specs=[SMEM, SMEM] + [VMEM] * 5 + [pl.BlockSpec(memory_space=pl.ANY)] * 3,
        out_specs=pl.BlockSpec(memory_space=pl.ANY),
        scratch_shapes=[
            pltpu.VMEM((3, samples, width), BF16),
            pltpu.VMEM((positions, width, width), F32),
            pltpu.SemaphoreType.DMA((3,)),
            pltpu.SemaphoreType.DMA((positions, 2)),
        ],
        compiler_params=limit(32),
    )(number, over, trace, counts, right, tiles, diagonal, *eights)


def helper_pairs(rows_count, cols_count):
    fine, half_rows = cols_count // COARSE, rows_count // 2
    pairs = []
    for row in range(rows_count):
        half = row // half_rows
        for tile in range(cols_count):
            wanted = tile == 0 or (tile // fine % 2 == half and not (half == 1 and tile == fine))
            if wanted:
                helper = tile + fine * (1 - 2 * (tile // fine % 2))
                pairs.append((row * cols_count + tile, row * cols_count + helper))
    return pairs


def eight_pairs(rows_count, cols_count):
    fine = cols_count // COARSE
    wanted = rows_count // 2 * cols_count
    first = [(fine, wanted)]
    return first, [
        [(row * cols_count + fine, wanted + 2 * row + turn) for row in range(rows_count) if row + turn > 0] for turn in range(2)
    ]


def per_device(samples, counts, shrink_num, shrink_den):
    rows_count = lax.axis_size("row")
    cols_count = lax.axis_size("col")
    rows, width = samples.shape
    taps = width * cols_count
    both = ("row", "col")
    helped = lax.ppermute(samples, both, helper_pairs(rows_count, cols_count))
    counts = counts[None, :]
    gathered = lax.all_to_all(copies(samples, rows_count), "row", 0, 0)
    scaled, pieces = scale(weigh(counts), gathered, helped, cols_count)
    pairs_first, pairs_late = eight_pairs(rows_count, cols_count)
    eights = [lax.ppermute(gathered.reshape(rows_count * rows, width), both, pairs_first)]
    exchanged = lax.all_to_all(pieces, "col", 0, 0)
    half_rows = rows_count // 2
    dealt, trace = deal(exchanged, rows, width, half_rows)
    halves = [list(range(half_rows)), list(range(half_rows, rows_count))]
    dealt = lax.all_to_all(dealt, "row", 0, 0, axis_index_groups=halves)
    below, diagonal = panel(shrink_num, shrink_den, trace, scaled, taps)
    whole = hold(gathered, below)
    eights += [lax.ppermute(whole, both, pairs) for pairs in pairs_late]
    right, tiles = right_factor(shrink_num, shrink_den, trace, counts, below, dealt, taps)
    return finish(shrink_num, shrink_den, trace, counts, right, tiles, diagonal, eights, taps)


def solution(mesh):
    in_specs = (P("row", "col"), P(), P(), P())
    out_specs = P(None, "row", "col")
    return jax.shard_map(
        per_device, mesh=mesh, in_specs=in_specs, out_specs=out_specs, check_vma=False
    )
```

```python
import functools

import jax
import jax.numpy as jnp
from jax import lax
from jax.experimental import pallas as pl
from jax.experimental.pallas import tpu as pltpu
from jax.sharding import PartitionSpec as P

BLOCK = 128
MICRO = 32
STRIP = 16
TAIL = 8
COARSE = 4
F32 = jnp.float32
BF16 = jnp.bfloat16
VMEM = pl.BlockSpec(memory_space=pltpu.VMEM)
SMEM = pl.BlockSpec(memory_space=pltpu.SMEM)


def dot(left, right, dims, precision=None):
    return lax.dot_general(
        left, right, ((dims[0], dims[1]), ((), ())),
        precision=precision, preferred_element_type=F32,
    )


def split(value):
    high = value.astype(BF16)
    return high, (value - high.astype(F32)).astype(BF16)


def thirds(value):
    high, rest = value.astype(BF16), value
    rest = rest - high.astype(F32)
    middle = rest.astype(BF16)
    return high, middle, (rest - middle.astype(F32)).astype(BF16)


def stack(parts, order, axis):
    return jnp.concatenate([parts[which] for which in order], axis=axis)


LEFT, RIGHT = (0, 0, 1, 0, 1, 2), (0, 1, 0, 2, 1, 0)


def gram(value, first, last):
    parts = thirds(value)
    left = stack([part[:, first:last] for part in parts], LEFT, 0)
    return dot(left, stack(parts, RIGHT, 0), ((0,), (0,)))


def short_gram(value):
    parts = split(value)
    return dot(stack(parts, (0, 0, 1), 0), stack(parts, (0, 1, 0), 0), ((0,), (0,)))


def product(left, right):
    return dot(stack(thirds(left), LEFT, 1), stack(thirds(right), RIGHT, 0), ((1,), (0,)))


def copies_kernel(samples_ref, copies_ref):
    for target in range(copies_ref.shape[0]):
        copies_ref[target] = samples_ref[...]


def columns_of(counts):
    counts = counts.astype(F32)
    weights = jnp.broadcast_to(counts / jnp.sum(counts), (128, counts.shape[1]))
    return jnp.transpose(weights)


def scale_tile(weights, roots, samples):
    repeats = samples.shape[1] // 128
    values = samples.astype(F32)
    mean = jnp.sum(jnp.concatenate([weights] * repeats, axis=1) * values, axis=0, keepdims=True)
    return (jnp.concatenate([roots] * repeats, axis=1) * (values - mean)).astype(BF16)


def weights_kernel(counts_ref, weights_ref):
    weights = columns_of(counts_ref[...])
    weights_ref[0] = weights
    weights_ref[1] = jnp.sqrt(weights)


def scale_kernel(weights_ref, samples_ref, helped_ref, scaled_ref, pieces_ref):
    count, rows, width = samples_ref.shape
    scaled = scale_tile(weights_ref[0], weights_ref[1], samples_ref[...].reshape(count * rows, width))
    scaled_ref[...] = scaled
    share = jnp.sum(jnp.square(scaled.astype(F32)), axis=0, keepdims=True)
    share = jnp.broadcast_to(jnp.sum(share, axis=1, keepdims=True), (TAIL, 128))
    high, middle = split(share)
    low = (share - high.astype(F32) - middle.astype(F32)).astype(BF16)
    line = lax.broadcasted_iota(jnp.int32, (TAIL, 128), 0)
    tail = jnp.where(line == 0, high.astype(F32), 0.0)
    tail = jnp.where(line == 1, middle.astype(F32), tail)
    tail = jnp.where(line == 2, low.astype(F32), tail).astype(BF16)
    row = lax.axis_index("row")
    half = row // (count // 2)
    column = lax.axis_index("col")
    fine = pieces_ref.shape[0] // COARSE
    own = lax.rem(column // fine, 2) == half
    own = (column == 0) | (own & ((half == 0) | (column != fine)))
    other_block = samples_ref[lax.rem(row + count // 2, count)].astype(F32)
    sent = jnp.where(own, other_block, helped_ref[...].astype(F32)).astype(BF16)
    body = pieces_ref.shape[1] - TAIL
    for target in range(pieces_ref.shape[0]):
        for part in range(width // 128):
            pieces_ref[target, part * rows:(part + 1) * rows, :] = sent[:, part * 128:(part + 1) * 128]
        pieces_ref[target, body:, :] = tail


def deal_kernel(pieces_ref, dealt_ref, trace_ref):
    columns, high, _ = pieces_ref.shape
    targets, dealt_rows, width = dealt_ref.shape
    fine = columns // COARSE
    rows = dealt_rows // 6
    half = lax.axis_index("row") // targets
    for target in range(targets):
        sources = ((1 - half) * fine, half * fine, fine + target, target, 3 * fine + target, 2 * fine + target)
        for place, source in enumerate(sources):
            for part in range(width // 128):
                dealt_ref[target, place * rows:(place + 1) * rows, part * 128:(part + 1) * 128] = pieces_ref[
                    source, part * rows:(part + 1) * rows, :
                ]
    total = jnp.zeros((TAIL, 128), F32)
    for column in range(columns):
        total = total + pieces_ref[column, high - TAIL:, :].astype(F32)
    trace_ref[...] = jnp.broadcast_to(jnp.sum(total, axis=0, keepdims=True), (8, 128))


def eliminate(work_ref, first, micro):
    lanes = work_ref.shape[1]
    groups = micro // 8
    rows = [[work_ref[first + 8 * g:first + 8 * g + 8, 128 * w:128 * w + 128] for w in range(lanes // 128)] for g in range(groups)]
    part, lane = first // 128, first % 128
    for begin in range(0, micro, STRIP):
        columns = {
            k: {g: jnp.broadcast_to(rows[g][part][:, lane + k:lane + k + 1], (8, 128)) for g in range(begin // 8, groups)}
            for k in range(begin, begin + STRIP)
        }
        for j in range(begin, begin + STRIP):
            group, line = j // 8, j % 8

            def spread(value):
                return jnp.broadcast_to(value[line:line + 1, :], (8, 128))

            pivot = spread(columns[j][group])
            inverse = 1.0 / pivot
            scale = lax.rsqrt(pivot)
            live = range((j + 1) // 8, groups)
            multiplier = {g: columns[j][g] * inverse for g in live}
            for k in range(j + 1, begin + STRIP):
                entry = spread(columns[k][group])
                for g in live:
                    columns[k][g] = columns[k][g] - multiplier[g] * entry
            for w in range(lanes // 128):
                entry = spread(rows[group][w])
                work_ref[first + j:first + j + 1, 128 * w:128 * w + 128] = (entry * scale)[0:1, :]
                for g in live:
                    rows[g][w] = rows[g][w] - multiplier[g] * entry


def factor_block(work_ref, block, micro):
    for first in range(0, block, micro):
        eliminate(work_ref, first, micro)
        after = first + micro
        if after < block:
            panel = work_ref[first:after, :]
            work_ref[after:, :] = work_ref[after:, :] - gram(panel, after, block)


def identity(size):
    return jnp.where(
        lax.broadcasted_iota(jnp.int32, (size, size), 0) == lax.broadcasted_iota(jnp.int32, (size, size), 1), 1.0, 0.0
    ).astype(F32)


def factor_panel(panel_ref, work_ref, order):
    for start in range(0, order, BLOCK):
        stop = start + BLOCK
        work_ref[:, 0:BLOCK] = panel_ref[start:stop, start:stop]
        work_ref[:, BLOCK:] = identity(BLOCK)
        factor_block(work_ref, BLOCK, MICRO)
        panel_ref[start:stop, start:stop] = work_ref[:, 0:BLOCK]
        done = product(work_ref[:, BLOCK:], panel_ref[start:stop, stop:])
        panel_ref[start:stop, stop:] = done
        if stop < order:
            panel_ref[stop:order, stop:] = panel_ref[stop:order, stop:] - gram(done, 0, order - stop)


def coefficients(number_ref, over_ref, trace_ref, taps):
    shrinkage = number_ref[0].astype(F32) / over_ref[0].astype(F32)
    return 1.0 - shrinkage, shrinkage * trace_ref[0:1, 0:1] / taps


def panel_kernel(taps, number_ref, over_ref, trace_ref, scaled_ref, below_ref, diagonal_ref, panel_ref, work_ref):
    width = scaled_ref.shape[1]

    @pl.when(lax.axis_index("col") > 0)
    def _():
        below_ref[...] = scaled_ref[...].astype(F32)

    @pl.when(lax.axis_index("col") == 0)
    def _():
        keep, level = coefficients(number_ref, over_ref, trace_ref, taps)
        own = scaled_ref[...]
        panel_ref[:, 0:width] = (keep / level) * dot(own, own, ((0,), (0,))) + identity(width)
        panel_ref[:, width:] = jnp.transpose(own.astype(F32))
        factor_panel(panel_ref, work_ref, width)
        root = jnp.sqrt(level)
        below_ref[...] = jnp.transpose(panel_ref[:, width:]) * (keep / root)
        line = lax.broadcasted_iota(jnp.int32, (width, width), 0)
        lane = lax.broadcasted_iota(jnp.int32, (width, width), 1)
        diagonal_ref[...] = jnp.transpose(jnp.where(line <= lane, panel_ref[:, 0:width], 0.0)) * root


def right_kernel(
    taps, number_ref, over_ref, trace_ref, counts_ref, below_ref, dealt_ref, right_ref, tiles_ref, panel_ref, work_ref
):
    samples, width = below_ref.shape
    rows = samples // dealt_ref.shape[0]
    weights = columns_of(counts_ref[...])
    roots = jnp.sqrt(weights)

    def tile(place):
        halves = [
            dealt_ref[:, start:start + rows // 2, :].reshape(samples // 2, width)
            for start in (place * rows, place * rows + rows // 2)
        ]
        return scale_tile(weights, roots, jnp.concatenate(halves, axis=0))

    def fill():
        for position in range(tiles_ref.shape[0]):
            tiles_ref[position] = tile(position + 1)

    @pl.when(lax.axis_index("col") == 0)
    def _():
        right_ref[...] = jnp.concatenate(split(below_ref[...]), axis=0)
        fill()

    @pl.when(lax.axis_index("col") > 0)
    def _():
        keep, level = coefficients(number_ref, over_ref, trace_ref, taps)
        first_tile = tile(0)
        panel_ref[:, 0:samples] = (keep / level) * dot(first_tile, first_tile, ((1,), (1,))) + identity(samples)
        panel_ref[:, samples:] = identity(samples)
        factor_panel(panel_ref, work_ref, samples)
        fill()
        inverse_factor = panel_ref[:, samples:]
        parts = jnp.concatenate(split(keep * short_gram(inverse_factor)), axis=1)
        own = below_ref[...].astype(BF16)
        right_ref[...] = jnp.concatenate(split(dot(parts, jnp.concatenate([own, own], axis=0), ((1,), (0,)))), axis=0)


def finish_kernel(
    taps, number_ref, over_ref, trace_ref, counts_ref, right_ref, tiles_ref, diagonal_ref, eight_ref, even_ref, odd_ref, out_ref,
    held_ref, made_ref, arrived, sent,
):
    positions, samples, width = tiles_ref.shape
    row_index, col_index = lax.axis_index("row"), lax.axis_index("col")
    rows_count = lax.axis_size("row")
    step = width // 2
    moves = []

    def fill(position, start, tile):
        part = tile[:, start:start + step]
        made_ref[position, start:start + step, :] = dot(jnp.concatenate([part, part], axis=0), right_ref[...], ((0,), (0,)))

    def send(position, start):
        @pl.when((position * rows_count + row_index == col_index) & (col_index > 0))
        def _():
            _, level = coefficients(number_ref, over_ref, trace_ref, taps)
            made_ref[position, start:start + step, start:start + step] = (
                made_ref[position, start:start + step, start:start + step] + level * identity(step)
            )
        move = pltpu.make_async_copy(
            made_ref.at[position, pl.ds(start, step)], out_ref.at[position, pl.ds(start, step)], sent.at[position, start // step]
        )
        move.start()
        moves.append(move)

    for start in (0, step):
        fill(1, start, tiles_ref[1])
        send(1, start)

    eighth = 2 * row_index == rows_count

    @pl.when(eighth)
    def _():
        copies_in = [
            pltpu.make_async_copy(source, held_ref.at[place], arrived.at[place])
            for place, source in enumerate((eight_ref, even_ref, odd_ref))
        ]
        for copy in copies_in:
            copy.start()
        for copy in copies_in:
            copy.wait()
        weights = columns_of(counts_ref[...])
        eight = held_ref[0].astype(F32) + held_ref[1].astype(F32) + held_ref[2].astype(F32)
        held_ref[0] = scale_tile(weights, jnp.sqrt(weights), eight)

    for start in (0, step):
        @pl.when(eighth)
        def _():
            fill(0, start, held_ref[0])

        @pl.when(jnp.logical_not(eighth) & (row_index > 0))
        def _():
            fill(0, start, tiles_ref[0])

        @pl.when((row_index == 0) & (col_index > 0))
        def _():
            made_ref[0, start:start + step, :] = jnp.zeros((step, width), F32)

        @pl.when((row_index == 0) & (col_index == 0))
        def _():
            made_ref[0, start:start + step, :] = diagonal_ref[start:start + step, :]

        send(0, start)

    for move in moves:
        move.wait()


def limit(mebibytes):
    return pltpu.CompilerParams(vmem_limit_bytes=mebibytes * 2**20)


def copies(samples, count):
    return pl.pallas_call(
        copies_kernel,
        out_shape=jax.ShapeDtypeStruct((count, *samples.shape), BF16),
        in_specs=[VMEM],
        out_specs=VMEM,
        compiler_params=limit(8),
    )(samples)


def weigh(counts):
    return pl.pallas_call(
        weights_kernel,
        out_shape=jax.ShapeDtypeStruct((2, counts.shape[1], 128), F32),
        in_specs=[VMEM],
        out_specs=VMEM,
        compiler_params=limit(8),
        cost_estimate=pl.CostEstimate(flops=2 * 10**9, bytes_accessed=2 * 2**20, transcendentals=0),
    )(counts)


def scale(weights, gathered, helped, columns):
    count, rows, width = gathered.shape
    return pl.pallas_call(
        scale_kernel,
        out_shape=(
            jax.ShapeDtypeStruct((count * rows, width), BF16),
            jax.ShapeDtypeStruct((columns, rows * width // 128 + TAIL, 128), BF16),
        ),
        in_specs=[VMEM] * 3,
        out_specs=(VMEM, VMEM),
        compiler_params=limit(16),
    )(weights, gathered, helped)


def deal(pieces, rows, width, targets):
    return pl.pallas_call(
        deal_kernel,
        out_shape=(
            jax.ShapeDtypeStruct((targets, 6 * rows, width), BF16),
            jax.ShapeDtypeStruct((8, 128), F32),
        ),
        in_specs=[VMEM],
        out_specs=(VMEM, VMEM),
        compiler_params=limit(16),
    )(pieces)


def hold_kernel(_, value_ref, held_ref):
    count, rows, _ = value_ref.shape
    held_ref[...] = value_ref[...].reshape(count * rows, -1)


def hold(value, after):
    count, rows, width = value.shape
    return pl.pallas_call(
        hold_kernel,
        out_shape=jax.ShapeDtypeStruct((count * rows, width), BF16),
        in_specs=[pl.BlockSpec(memory_space=pl.ANY), VMEM],
        out_specs=VMEM,
        compiler_params=limit(8),
    )(after, value)


def panel(number, over, trace, scaled, taps):
    samples, width = scaled.shape
    return pl.pallas_call(
        functools.partial(panel_kernel, taps),
        out_shape=(
            jax.ShapeDtypeStruct((samples, width), F32),
            jax.ShapeDtypeStruct((width, width), F32),
        ),
        in_specs=[SMEM, SMEM, VMEM, VMEM],
        out_specs=(VMEM, VMEM),
        scratch_shapes=[
            pltpu.VMEM((width, width + samples), F32),
            pltpu.VMEM((BLOCK, 2 * BLOCK), F32),
        ],
        compiler_params=limit(32),
        cost_estimate=pl.CostEstimate(flops=20 * 10**9, bytes_accessed=2 * 2**20, transcendentals=0),
    )(number, over, trace, scaled)


def right_factor(number, over, trace, counts, below, dealt, taps):
    samples, width = below.shape
    return pl.pallas_call(
        functools.partial(right_kernel, taps),
        out_shape=(
            jax.ShapeDtypeStruct((2 * samples, width), BF16),
            jax.ShapeDtypeStruct((2, samples, width), BF16),
        ),
        in_specs=[SMEM, SMEM] + [VMEM] * 4,
        out_specs=(VMEM, VMEM),
        scratch_shapes=[
            pltpu.VMEM((samples, 2 * samples), F32),
            pltpu.VMEM((BLOCK, 2 * BLOCK), F32),
        ],
        compiler_params=limit(32),
        cost_estimate=pl.CostEstimate(flops=10**10, bytes_accessed=2 * 2**20, transcendentals=0),
    )(number, over, trace, counts, below, dealt)


def finish(number, over, trace, counts, right, tiles, diagonal, eights, taps):
    positions, samples, width = tiles.shape
    return pl.pallas_call(
        functools.partial(finish_kernel, taps),
        out_shape=jax.ShapeDtypeStruct((positions, width, width), F32),
        in_specs=[SMEM, SMEM] + [VMEM] * 5 + [pl.BlockSpec(memory_space=pl.ANY)] * 3,
        out_specs=pl.BlockSpec(memory_space=pl.ANY),
        scratch_shapes=[
            pltpu.VMEM((3, samples, width), BF16),
            pltpu.VMEM((positions, width, width), F32),
            pltpu.SemaphoreType.DMA((3,)),
            pltpu.SemaphoreType.DMA((positions, 2)),
        ],
        compiler_params=limit(32),
    )(number, over, trace, counts, right, tiles, diagonal, *eights)


def helper_pairs(rows_count, cols_count):
    fine, half_rows = cols_count // COARSE, rows_count // 2
    pairs = []
    for row in range(rows_count):
        half = row // half_rows
        for tile in range(cols_count):
            wanted = tile == 0 or (tile // fine % 2 == half and not (half == 1 and tile == fine))
            if wanted:
                helper = tile + fine * (1 - 2 * (tile // fine % 2))
                pairs.append((row * cols_count + tile, row * cols_count + helper))
    return pairs


def eight_pairs(rows_count, cols_count):
    fine = cols_count // COARSE
    wanted = rows_count // 2 * cols_count
    first = [(fine, wanted)]
    return first, [
        [(row * cols_count + fine, wanted + 2 * row + turn) for row in range(rows_count) if row + turn > 0] for turn in range(2)
    ]


def per_device(samples, counts, shrink_num, shrink_den):
    rows_count = lax.axis_size("row")
    cols_count = lax.axis_size("col")
    rows, width = samples.shape
    taps = width * cols_count
    both = ("row", "col")
    helped = lax.ppermute(samples, both, helper_pairs(rows_count, cols_count))
    counts = counts[None, :]
    gathered = lax.all_to_all(copies(samples, rows_count), "row", 0, 0)
    scaled, pieces = scale(weigh(counts), gathered, helped, cols_count)
    pairs_first, pairs_late = eight_pairs(rows_count, cols_count)
    eights = [lax.ppermute(gathered.reshape(rows_count * rows, width), both, pairs_first)]
    exchanged = lax.all_to_all(pieces, "col", 0, 0)
    half_rows = rows_count // 2
    dealt, trace = deal(exchanged, rows, width, half_rows)
    halves = [list(range(half_rows)), list(range(half_rows, rows_count))]
    dealt = lax.all_to_all(dealt, "row", 0, 0, axis_index_groups=halves)
    below, diagonal = panel(shrink_num, shrink_den, trace, scaled, taps)
    whole = hold(gathered, below)
    eights += [lax.ppermute(whole, both, pairs) for pairs in pairs_late]
    right, tiles = right_factor(shrink_num, shrink_den, trace, counts, below, dealt, taps)
    return finish(shrink_num, shrink_den, trace, counts, right, tiles, diagonal, eights, taps)


def solution(mesh):
    in_specs = (P("row", "col"), P(), P(), P())
    out_specs = P(None, "row", "col")
    return jax.shard_map(
        per_device, mesh=mesh, in_specs=in_specs, out_specs=out_specs, check_vma=False
    )
```
